32 devices in a mesh: section: 2 (over core), ctx: 4 (over z), fsdp: 4 (over y, x).
Axes of the slice: x: 2, y: 2, z: 4, core: 2. Of those that a mesh axis runs over, the one named last changes fastest.
Arguments:
- inputs: bfloat16 [2, 4, 1024, 576], P(None, 'fsdp', 'ctx'), may hold values from -6 to 6
- positions: int32 [2, 4, 1024], P(None, 'fsdp', 'ctx'), may hold values from 0 to 1023, as said below
- out_grad: bfloat16 [2, 4, 1024, 576], P(None, 'fsdp', 'ctx'), may hold values from -6 to 6
- attn_gain: bfloat16 [2, 576], P('section', 'fsdp'), may hold values from 0.5 to 1.5
- query_proj: bfloat16 [2, 576, 576], P('section', 'fsdp'), may hold values from -0.25 to 0.25
- key_proj: bfloat16 [2, 576, 192], P('section', 'fsdp'), may hold values from -0.25 to 0.25
- value_proj: bfloat16 [2, 576, 192], P('section', 'fsdp'), may hold values from -0.25 to 0.25
- out_proj: bfloat16 [2, 576, 576], P('section', 'fsdp'), may hold values from -2 to 2
- mlp_gain: bfloat16 [2, 576], P('section', 'fsdp'), may hold values from 0.5 to 1.5
- gate_proj: bfloat16 [2, 576, 1536], P('section', 'fsdp'), may hold values from -0.25 to 0.25
- up_proj: bfloat16 [2, 576, 1536], P('section', 'fsdp'), may hold values from -0.25 to 0.25
- down_proj: bfloat16 [2, 1536, 576], P('section', 'fsdp'), may hold values from -0.15625 to 0.15625
Outputs:
- section_out: bfloat16 [2, 2, 4, 1024, 576], P('section', None, 'fsdp', 'ctx')
- input_grad: bfloat16 [2, 2, 4, 1024, 576], P('section', None, 'fsdp', 'ctx')
- attn_gain_grad: float32 [2, 576], P('section', 'fsdp')
- query_proj_grad: float32 [2, 576, 576], P('section', 'fsdp')
- key_proj_grad: float32 [2, 576, 192], P('section', 'fsdp')
- value_proj_grad: float32 [2, 576, 192], P('section', 'fsdp')
- out_proj_grad: float32 [2, 576, 576], P('section', 'fsdp')
- mlp_gain_grad: float32 [2, 576], P('section', 'fsdp')
- gate_proj_grad: float32 [2, 576, 1536], P('section', 'fsdp')
- up_proj_grad: float32 [2, 576, 1536], P('section', 'fsdp')
- down_proj_grad: float32 [2, 1536, 576], P('section', 'fsdp')
The draws below stay inside these ranges and needn't reach their ends.
Inputs may be any that keep to these rules, and one draw needn't show every extreme that they name: `positions`: along each sequence a position counts up by one from 0 at the start of each document; in every draw some sequence is one document of 1024 tokens.
All inputs are finite; a program needn't handle non-finite values.
Results may differ from the reference program's by a relative error of at most 0.03.
Values may be sent and summed in bfloat16 or wider, within the bound.
No kernel may reach another device: no remote copies, remote signals or barrier semaphores. Data moves between devices by JAX's collectives and lax.ppermute only.
A program may use at most 192 MiB of HBM per device.

```python
import jax
import jax.numpy as jnp
from jax import lax

D = 576
HQ = 9
HK = 3
HD = 64
FF = 1536
LEN = 1024
MICRO = 2
SEQS = 4


def draw_positions(key, part):
    key = jax.random.fold_in(key, 7)
    flag_key, pick_key = jax.random.split(key)
    seq_total = MICRO * SEQS
    steps_here = jnp.arange(LEN, dtype=jnp.int32)
    starts = jax.random.randint(flag_key, (seq_total, LEN), 0, LEN) < 2
    starts = starts | (steps_here == 0)[None, :]
    single = jax.random.randint(pick_key, (), 0, seq_total)
    lone_mask = (jnp.arange(seq_total, dtype=jnp.int32)[:, None] == single) & (steps_here[None, :] > 0)
    starts = starts & jnp.logical_not(lone_mask)
    last_start = lax.cummax(jnp.where(starts, steps_here[None, :], 0), axis=1)
    return (steps_here[None, :] - last_start).reshape(MICRO, SEQS, LEN).astype(jnp.int32)


def spiked(result, own_key, source, target, parts, factor):
    def block_of(position):
        return (jnp.arange(result.shape[position]) // (result.shape[position] // parts)).reshape((-1,) + (1,) * (result.ndim - 1 - position))

    near = jax.random.permutation(own_key, parts)[block_of(target)]
    other_side = (block_of(target) + parts // 2) % parts
    return jnp.where((block_of(source) == near) | (block_of(source) == other_side), factor * result, result)


def block_scale(key, dims, cuts, smallest, high):
    def one(axis_at, parts):
        draws = jax.random.uniform(jax.random.fold_in(jax.random.fold_in(key, 6), axis_at), (parts,), jnp.float32, smallest / len(cuts), high / len(cuts))
        return jnp.repeat(jnp.exp(draws), dims[axis_at] // parts).reshape((-1,) + (1,) * (len(dims) - axis_at - 1))

    level = one(*cuts[0])
    for cut in cuts[1:]:
        level = level * one(*cut)
    return level


def gaussian(own_key, extent, scale, reach, cuts=(), kind=jnp.bfloat16):
    entries = jax.random.normal(own_key, extent, jnp.float32) * scale
    if len(cuts) > 0:
        entries = block_scale(own_key, extent, cuts, -0.22, 0.18) * entries
    return jnp.clip(entries, min=-reach, max=reach).astype(kind)


def gaussian_with(rng, shape, deviation, bound, cuts, heavy, kind=jnp.bfloat16):
    values = deviation * jax.random.normal(rng, shape, jnp.float32)
    if cuts:
        values = values * block_scale(rng, shape, cuts, -0.22, 0.18)
    return jnp.clip(spiked(values, jax.random.fold_in(rng, 3), *heavy), -bound, bound).astype(kind)


def setup_inputs(seed: int = 0) -> dict:
    key_list = jax.random.split(jax.random.key(seed), 13)
    inputs = gaussian_with(key_list[0], (MICRO, SEQS, LEN, D), 1.0, 6.0, ((1, 4), (2, 4)), (1, 3, 4, 2.0))
    positions = draw_positions(jax.random.fold_in(key_list[12], 71), 0)
    out_grad = gaussian(key_list[2], (MICRO, SEQS, LEN, D), 1.0, 6.0, ((1, 4), (2, 4)))
    attn_gain = jnp.clip(1.0 + 0.1 * jax.random.normal(key_list[3], (2, D), jnp.float32), 0.5, 1.5).astype(jnp.bfloat16)
    query_proj = gaussian(key_list[4], (2, D, HQ * HD), D ** -0.5, 0.25, ((0, 2), (1, 4)))
    key_proj = gaussian(key_list[5], (2, D, HK * HD), D ** -0.5, 0.25, ((0, 2), (1, 4)))
    value_proj = gaussian(key_list[6], (2, D, HK * HD), D ** -0.5, 0.25, ((0, 2), (1, 4)))
    out_proj = gaussian(key_list[7], (2, HQ * HD, D), (D // 64) ** -0.5, 2.0, ((0, 2), (1, 4)))
    mlp_gain = jnp.clip(1.0 + 0.1 * jax.random.normal(key_list[8], (2, D), jnp.float32), 0.5, 1.5).astype(jnp.bfloat16)
    gate_proj = gaussian(key_list[9], (2, D, FF), D ** -0.5, 0.25, ((0, 2), (1, 4)))
    up_proj = gaussian(key_list[10], (2, D, FF), D ** -0.5, 0.25, ((0, 2), (1, 4)))
    down_proj = gaussian(key_list[11], (2, FF, D), FF ** -0.5, 0.15625, ((0, 2), (1, 4)))
    return dict(inputs=inputs, positions=positions, out_grad=out_grad, attn_gain=attn_gain, query_proj=query_proj, key_proj=key_proj, value_proj=value_proj, out_proj=out_proj, mlp_gain=mlp_gain, gate_proj=gate_proj, up_proj=up_proj, down_proj=down_proj)


@jax.custom_vjp
def low(v):
    return lax.optimization_barrier(v.astype(jnp.bfloat16)).astype(jnp.float32)

@jax.custom_vjp
def low_back(v):
    return v

def low_keep(v):
    return (low(v), None)

def low_pass(kept, grad):
    return (grad,)

def back_keep(v):
    return (v, None)

def back_low(kept, grad):
    return (low(grad),)
low.defvjp(low_keep, low_pass)
low_back.defvjp(back_keep, back_low)
epsilon = 1e-05
rope_base = 100000.0
masked_score = -1e+30

def project(features, matrix):
    return jnp.einsum('bld,df->blf', features, matrix, precision=lax.Precision.HIGHEST)

def rms_normed(features, gain_vec):
    return features * lax.rsqrt(lax.optimization_barrier(jnp.mean(features * features, axis=-1, keepdims=True)) + epsilon) * gain_vec

def rope_tables(places):
    frequency = rope_base ** (-(jnp.arange(HD // 2, dtype=jnp.float32) * 2.0 / HD))
    angles = places.astype(jnp.float32)[..., None] * frequency
    angles = jnp.concatenate([angles, angles], axis=-1)[..., None, :]
    return (jnp.cos(angles), jnp.sin(angles))

def rotate(features, cosine_table, sine_table):
    half_size = features.shape[-1] // 2
    turned = jnp.concatenate([-features[..., half_size:], features[..., :half_size]], axis=-1)
    return features * cosine_table + turned * sine_table

def attention(query_matrix, key_heads, value_heads):
    batch_size, length = (query_matrix.shape[0], query_matrix.shape[1])
    grouped = query_matrix.reshape(batch_size, length, HK, HQ // HK, HD).transpose(0, 2, 3, 1, 4)
    block_rows = min(512, length)
    block_count = length // block_rows
    blocks = grouped.reshape(batch_size, HK, HQ // HK, block_count, block_rows, HD).transpose(3, 0, 1, 2, 4, 5)
    first_rows = jnp.arange(block_count, dtype=jnp.int32) * block_rows
    columns = jnp.arange(length, dtype=jnp.int32)

    @jax.checkpoint
    def one_block(item_pair):
        block_queries, first_row = item_pair
        scores = jnp.einsum('bhgqd,bkhd->bhgqk', block_queries, key_heads, precision=lax.Precision.HIGHEST)
        scores = low_back(scores * HD ** (-0.5))
        rows_here = first_row + jnp.arange(block_rows, dtype=jnp.int32)
        scores = jnp.where(rows_here[:, None] >= columns[None, :], scores, masked_score)
        probabilities = jax.nn.softmax(scores, axis=-1)
        return jnp.einsum('bhgqk,bkhd->bhgqd', low(probabilities), value_heads, precision=lax.Precision.HIGHEST)
    outputs = lax.map(one_block, (blocks, first_rows))
    return outputs.transpose(1, 0, 4, 2, 3, 5).reshape(batch_size, length, HQ, HD)

def layer(features, params, places):
    attn_gain, query_proj, key_proj, value_proj, out_proj, mlp_gain, gate_proj, up_proj, down_proj = params
    batch_size, length, model_width = features.shape
    cosine_table, sine_table = rope_tables(places)
    normalized_rows = low(rms_normed(features, attn_gain))
    query_matrix = low(rotate(low_back(project(normalized_rows, query_proj)).reshape(batch_size, length, HQ, HD), cosine_table, sine_table))
    key_heads = low(rotate(low_back(project(normalized_rows, key_proj)).reshape(batch_size, length, HK, HD), cosine_table, sine_table))
    value_heads = low(low_back(project(normalized_rows, value_proj))).reshape(batch_size, length, HK, HD)
    attended = attention(query_matrix, key_heads, value_heads)
    attn_rows = low(low_back(attended)).reshape(batch_size, length, HQ * HD)
    resid = features + low_back(project(attn_rows, out_proj))
    mlp_normed = low(rms_normed(resid, mlp_gain))
    gate_vals = low_back(project(mlp_normed, gate_proj))
    up_vals = low_back(project(mlp_normed, up_proj))
    hidden = low(jax.nn.silu(gate_vals) * up_vals)
    return resid + low_back(project(hidden, down_proj))

def reference(inputs, positions, out_grad, attn_gain, query_proj, key_proj, value_proj, out_proj, mlp_gain, gate_proj, up_proj, down_proj):
    weight_list = (attn_gain, query_proj, key_proj, value_proj, out_proj, mlp_gain, gate_proj, up_proj, down_proj)
    first_params = tuple((element[0].astype(jnp.float32) for element in weight_list))
    second_params = tuple((element[1].astype(jnp.float32) for element in weight_list))
    seq_total = MICRO * SEQS
    group_size = max(1, min(seq_total, 4096 // LEN))
    while seq_total % group_size:
        group_size -= 1
    group_count = seq_total // group_size

    def regroup(tensor):
        return tensor.reshape((group_count, group_size) + tensor.shape[2:])

    def group_step(sums_so_far, group_data):
        block_in, places, block_grad = group_data

        def apply_layer(features, params):
            return layer(features, params, places)
        middle, first_back = jax.vjp(apply_layer, block_in.astype(jnp.float32), first_params)
        middle_low = low(middle)
        final_out, second_back = jax.vjp(apply_layer, middle_low, second_params)
        middle_grad, second_grads = second_back(block_grad.astype(jnp.float32))
        middle_grad = low(middle_grad)
        entry_grad, first_grads = first_back(middle_grad)
        first_sums = tuple((running + addition for running, addition in zip(sums_so_far[0], first_grads)))
        second_sums = tuple((running + addition for running, addition in zip(sums_so_far[1], second_grads)))
        return ((first_sums, second_sums), (middle_low, low(final_out), low(entry_grad), middle_grad))
    zero_sums = (tuple((jnp.zeros_like(element) for element in first_params)), tuple((jnp.zeros_like(element) for element in second_params)))
    sums_found, stacked = lax.scan(group_step, zero_sums, (regroup(inputs), regroup(positions), regroup(out_grad)))
    middles, finals, entry_grads, middle_grads = stacked
    full_shape = (MICRO, SEQS, LEN, D)
    section_out = jnp.stack([middles.reshape(full_shape), finals.reshape(full_shape)]).astype(jnp.bfloat16)
    input_grad = jnp.stack([entry_grads.reshape(full_shape), middle_grads.reshape(full_shape)]).astype(jnp.bfloat16)
    gradients = [jnp.stack([one_sum, two_sum]) for one_sum, two_sum in zip(sums_found[0], sums_found[1])]
    return (section_out, input_grad, gradients[0], gradients[1], gradients[2], gradients[3], gradients[4], gradients[5], gradients[6], gradients[7], gradients[8])
```

```python
import functools

import jax
import jax.numpy as jnp
from jax import lax
from jax.experimental import pallas as pl
from jax.experimental.pallas import tpu as pltpu
from jax.sharding import PartitionSpec as P

HQ = 9
HK = 3
HD = 64
GROUP = HQ // HK
LANES = 128

epsilon = 1e-05
rope_base = 100000.0
masked_score = -1e30

BF = jnp.bfloat16
F32 = jnp.float32
VMEM_LIMIT = 56 * 1024 * 1024

IN_VMEM = pl.BlockSpec(memory_space=pltpu.VMEM)
IN_SMEM = pl.BlockSpec(memory_space=pltpu.SMEM)
ANYWHERE = pl.BlockSpec(memory_space=pl.ANY)


def nn(a, b):
    return lax.dot_general(a, b, (((1,), (0,)), ((), ())), preferred_element_type=F32)


def nt(a, b):
    return lax.dot_general(a, b, (((1,), (1,)), ((), ())), preferred_element_type=F32)


def tn(a, b):
    return lax.dot_general(a, b, (((0,), (0,)), ((), ())), preferred_element_type=F32)


def shape(dims, kind):
    return jax.ShapeDtypeStruct(dims, kind)


def call(kernel, outs, in_specs, scratch, args, flops):
    moved = sum(a.size * a.dtype.itemsize for a in args)
    moved += sum(o.size * o.dtype.itemsize for o in outs)
    return pl.pallas_call(
        kernel,
        out_shape=tuple(outs),
        in_specs=in_specs,
        out_specs=tuple(IN_VMEM for _ in outs),
        scratch_shapes=scratch,
        compiler_params=pltpu.CompilerParams(vmem_limit_bytes=VMEM_LIMIT),
        cost_estimate=pl.CostEstimate(flops=flops, bytes_accessed=moved, transcendentals=0),
    )(*args)


def fetch(flag, yes_ref, no_ref, target, sem):
    @pl.when(flag)
    def _():
        pltpu.make_async_copy(yes_ref, target, sem).start()

    @pl.when(jnp.logical_not(flag))
    def _():
        pltpu.make_async_copy(no_ref, target, sem).start()


def arrive(ref, target, sem):
    pltpu.make_async_copy(ref, target, sem).wait()


def norm_scale(z):
    return lax.rsqrt(jnp.mean(z * z, axis=-1, keepdims=True) + epsilon)


def gain_row(tile):
    lane = lax.broadcasted_iota(jnp.int32, (8, LANES), 1)
    pick = jnp.where(lane == 0, 1.0, 0.0).astype(BF)
    return nt(pick, tile)[0:1]


def gain_tile(rows):
    return tn(rows.astype(BF), jnp.ones((rows.shape[0], LANES), BF)).astype(BF)


def wide(table, width):
    return jnp.concatenate([table] * (width // LANES), axis=1)


def low_half(width, rows):
    lane = lax.broadcasted_iota(jnp.int32, (rows, width), 1)
    return lax.rem(lane, HD) < HD // 2


def rot(a, cosine, sine):
    width = a.shape[1]
    up = pltpu.roll(a, HD // 2, 1)
    down = pltpu.roll(a, width - HD // 2, 1)
    turned = jnp.where(low_half(width, a.shape[0]), -down, up)
    return a * wide(cosine, width) + turned * wide(sine, width)


def rot_back(b, cosine, sine):
    width = b.shape[1]
    c = b * wide(sine, width)
    up = pltpu.roll(c, HD // 2, 1)
    down = pltpu.roll(c, width - HD // 2, 1)
    turned = jnp.where(low_half(width, b.shape[0]), down, -up)
    return b * wide(cosine, width) + turned


def attn_in_kernel(layer, idx, x, a_own, a_got, v_own, v_got, cos, sin, normed_out, q_out, kv_out, a_w, v_w, sems):
    own = idx[0] == layer
    fetch(own, a_own, a_got, a_w, sems.at[0])
    fetch(own, v_own, v_got, v_w, sems.at[1])
    z = x[...].astype(F32)
    scaled = z * norm_scale(z)
    arrive(a_own, a_w, sems.at[0])
    width = (HQ + HK) * HD
    gain = gain_row(a_w[:, width:])
    normed = (scaled * gain).astype(BF)
    normed_out[...] = normed
    qk = rot(nn(normed, a_w[:, :width]), cos[...], sin[...])
    q_out[...] = (qk[:, : HQ * HD].astype(BF).astype(F32) * HD ** (-0.5)).astype(BF)
    arrive(v_own, v_w, sems.at[1])
    value = nn(normed, v_w[:, :width])[:, HQ * HD :]
    kv_out[...] = jnp.concatenate([qk[:, HQ * HD :].astype(BF), value.astype(BF)], axis=1)


def attn_in(layer, idx, x, weights, cos, sin):
    rows, depth = x.shape
    a_own, a_got, v_own, v_got = weights
    args = (idx, x, a_own, a_got, v_own, v_got, cos, sin)
    return call(
        functools.partial(attn_in_kernel, layer),
        (shape((rows, depth), BF), shape((rows, HQ * HD), BF), shape((rows, 2 * HK * HD), BF)),
        [IN_SMEM, IN_VMEM] + [ANYWHERE] * 4 + [IN_VMEM] * 2,
        [pltpu.VMEM(a_own.shape, BF), pltpu.VMEM(v_own.shape, BF), pltpu.SemaphoreType.DMA((2,))],
        args,
        2 * rows * depth * 1536,
    )


def score_block(keys, query, block, reach, causal):
    s = nt(keys, query)
    if block == 0:
        return jnp.where(causal, s, masked_score)
    return jnp.where(block <= reach, s, masked_score)


def causal_mask(rows):
    key_at = lax.broadcasted_iota(jnp.int32, (rows, rows), 0)
    query_at = lax.broadcasted_iota(jnp.int32, (rows, rows), 1)
    return key_at <= query_at


def head(values, at):
    return values[:, at * HD : (at + 1) * HD]


def attend_kernel(blocks, idx, q, *refs):
    kv = [r[...] for r in refs[:blocks]]
    attn_out, lse_out = refs[blocks:]
    rows = q.shape[0]
    reach = idx[1]
    causal = causal_mask(rows)
    queries = q[...]
    pieces = []
    lse_out[...] = jnp.zeros_like(lse_out)
    for g in range(HK):
        keys = [head(b, g) for b in kv]
        values = jnp.concatenate([head(b, HK + g) for b in kv], axis=0)
        for i in range(GROUP):
            h = g * GROUP + i
            query = head(queries, h)
            s = jnp.concatenate(
                [score_block(k, query, d, reach, causal) for d, k in enumerate(keys)], axis=0
            )
            top = jnp.max(s, axis=0, keepdims=True)
            p = jnp.exp(s - top)
            total = jnp.sum(p, axis=0, keepdims=True)
            lse_out[h : h + 1, :] = top + jnp.log(total)
            p_low = (p * (1.0 / total)).astype(BF)
            pieces.append(tn(p_low, values).astype(BF))
    attn_out[...] = jnp.concatenate(pieces, axis=1)


def attend(idx, q, kv):
    rows = q.shape[0]
    return call(
        functools.partial(attend_kernel, len(kv)),
        (shape((rows, HQ * HD), BF), shape((16, rows), F32)),
        [IN_SMEM] + [IN_VMEM] * (1 + len(kv)),
        [],
        (idx, q) + tuple(kv),
        2 * 2 * rows * rows * len(kv) * HQ * HD * 4,
    )


def mlp_kernel(layer, idx, x, attn, v_own, v_got, g_m, g_t, d, y_out, resid_out, mn_out, gate_out, up_out, hid_out, v_w, sems):
    own = idx[0] == layer
    first = idx[0] == 0
    fetch(own, v_own, v_got, v_w, sems.at[0])
    arrive(v_own, v_w, sems.at[0])
    width = HQ * HD
    depth = x.shape[1]
    resid = x[...].astype(F32) + nn(attn[...], v_w[:, :depth])
    resid_out[...] = resid
    gain = gain_row(v_w[:, width + HK * HD :])
    mn = (resid * norm_scale(resid) * gain).astype(BF)
    mn_out[...] = mn
    mine = nn(mn, g_m[...])
    theirs = nn(mn, g_t[...])
    gate = jnp.where(first, mine, theirs)
    up = jnp.where(first, theirs, mine)
    gate_out[...] = gate
    up_out[...] = up
    hid = (gate * jax.nn.sigmoid(gate) * up).astype(BF)
    hid_out[...] = hid
    y_out[...] = (resid + nn(hid, d[...])).astype(BF)


def mlp(layer, idx, x, attn, weights, g_m, g_t, d):
    rows, depth = x.shape
    _, _, v_own, v_got = weights
    ff = g_m.shape[1]
    args = (idx, x, attn, v_own, v_got, g_m, g_t, d)
    return call(
        functools.partial(mlp_kernel, layer),
        (
            shape((rows, depth), BF),
            shape((rows, depth), F32),
            shape((rows, depth), BF),
            shape((rows, ff), F32),
            shape((rows, ff), F32),
            shape((rows, ff), BF),
        ),
        [IN_SMEM, IN_VMEM, IN_VMEM] + [ANYWHERE] * 2 + [IN_VMEM] * 3,
        [pltpu.VMEM(v_own.shape, BF), pltpu.SemaphoreType.DMA((1,))],
        args,
        2 * rows * depth * (3 * ff + depth),
    )


def mlp_back_kernel(layer, idx, e, resid, gate, up, g_m, g_t, d, v_own, v_got, gm_out, gt_out, rg_out, mix_out, ag_out, mg_out, v_w, sems):
    own = idx[0] == layer
    first = idx[0] == 0
    fetch(own, v_own, v_got, v_w, sems.at[0])
    low = e[...]
    hg = nt(low, d[...])
    gv = gate[...]
    sig = jax.nn.sigmoid(gv)
    g_in = (hg * up[...] * sig * (1.0 + gv * (1.0 - sig))).astype(BF)
    u_in = (hg * gv * sig).astype(BF)
    mine = jnp.where(first, g_in, u_in)
    theirs = jnp.where(first, u_in, g_in)
    gm_out[...] = mine
    gt_out[...] = theirs
    ng = nt(mine, g_m[...]) + nt(theirs, g_t[...])
    arrive(v_own, v_w, sems.at[0])
    width = HQ * HD
    depth = e.shape[1]
    gain = gain_row(v_w[:, width + HK * HD :])
    z = resid[...]
    inv = norm_scale(z)
    weighted = ng * gain
    mg_out[...] = gain_tile(ng * z * inv)
    part = inv * weighted - z * (inv * inv * inv) * jnp.mean(z * weighted, axis=-1, keepdims=True)
    rg = low.astype(F32) + part
    rg_out[...] = rg
    mix = rg.astype(BF)
    mix_out[...] = mix
    ag_out[...] = nt(mix, v_w[:, :depth]).astype(BF)


def mlp_back(layer, idx, e, resid, gate, up, g_m, g_t, d, weights):
    rows, depth = e.shape
    _, _, v_own, v_got = weights
    ff = g_m.shape[1]
    args = (idx, e, resid, gate, up, g_m, g_t, d, v_own, v_got)
    return call(
        functools.partial(mlp_back_kernel, layer),
        (
            shape((rows, ff), BF),
            shape((rows, ff), BF),
            shape((rows, depth), F32),
            shape((rows, depth), BF),
            shape((rows, HQ * HD), BF),
            shape((depth, LANES), BF),
        ),
        [IN_SMEM] + [IN_VMEM] * 7 + [ANYWHERE] * 2,
        [pltpu.VMEM(v_own.shape, BF), pltpu.SemaphoreType.DMA((1,))],
        args,
        2 * rows * depth * (3 * ff + depth),
    )


def mlp_grads_kernel(hid, e, mn, gm, gt, attn, mix, mg, ggm_out, ggt_out, dg_out, og_out):
    mnv = mn[...]
    ggm_out[...] = tn(mnv, gm[...]).astype(BF)
    ggt_out[...] = tn(mnv, gt[...]).astype(BF)
    dg_out[...] = tn(hid[...], e[...]).astype(BF)
    depth = mn.shape[1]
    width = (HQ + HK) * HD
    og_out[...] = jnp.zeros_like(og_out)
    og_out[:, :depth] = tn(attn[...], mix[...]).astype(BF)
    og_out[:, width:] = mg[...]


def mlp_grads(hid, e, mn, gm, gt, attn, mix, mg):
    rows, depth = e.shape
    ff = gm.shape[1]
    return call(
        mlp_grads_kernel,
        (
            shape((depth, ff), BF),
            shape((depth, ff), BF),
            shape((ff, depth), BF),
            shape((depth, (HQ + HK) * HD + LANES), BF),
        ),
        [IN_VMEM] * 8,
        [],
        (hid, e, mn, gm, gt, attn, mix, mg),
        2 * rows * depth * (3 * ff + depth),
    )


def attend_back_kernel(blocks, idx, q, ag, lse, *refs):
    kv = [r[...] for r in refs[:blocks]]
    dq_out, own_out = refs[blocks : blocks + 2]
    far_out = refs[blocks + 2 :]
    rows = q.shape[0]
    reach = idx[1]
    causal = causal_mask(rows)
    queries = q[...]
    grads = ag[...]
    dq_parts = []
    dk_parts = []
    dv_parts = []
    for g in range(HK):
        keys = [head(b, g) for b in kv]
        all_keys = jnp.concatenate(keys, axis=0)
        values = jnp.concatenate([head(b, HK + g) for b in kv], axis=0)
        dk = None
        dv = None
        for i in range(GROUP):
            h = g * GROUP + i
            query = head(queries, h)
            grad = head(grads, h)
            s = jnp.concatenate(
                [score_block(k, query, d, reach, causal) for d, k in enumerate(keys)], axis=0
            )
            p = jnp.exp(s - lse[h : h + 1, :])
            dp = nt(values, grad)
            delta = jnp.sum(p * dp, axis=0, keepdims=True)
            ds = (p * (dp - delta)).astype(BF)
            dv_h = nn(p.astype(BF), grad)
            dk_h = nn(ds, query)
            dk = dk_h if dk is None else dk + dk_h
            dv = dv_h if dv is None else dv + dv_h
            dq_parts.append(tn(ds, all_keys) * HD ** (-0.5))
        dk_parts.append(dk)
        dv_parts.append(dv)
    dq_out[...] = jnp.concatenate(dq_parts, axis=1)
    joined = jnp.concatenate(dk_parts + dv_parts, axis=1)
    own_out[...] = joined[:rows]
    for d, out in enumerate(far_out):
        out[...] = joined[(d + 1) * rows : (d + 2) * rows].astype(BF)


def attend_back(idx, q, ag, lse, kv):
    rows = q.shape[0]
    outs = [shape((rows, HQ * HD), F32), shape((rows, 2 * HK * HD), F32)]
    outs += [shape((rows, 2 * HK * HD), BF) for _ in kv[1:]]
    return call(
        functools.partial(attend_back_kernel, len(kv)),
        outs,
        [IN_SMEM] + [IN_VMEM] * (3 + len(kv)),
        [],
        (idx, q, ag, lse) + tuple(kv),
        5 * 2 * rows * rows * len(kv) * HQ * HD * 4,
    )


def input_back_kernel(layer, far, idx, x, normed, dq, own_kv, *refs):
    far_kv = refs[:far]
    rg, a_own, a_got, v_own, v_got, cos, sin, og, ig_out, m_out, t_out, a_w, v_w, sems = refs[far:]
    own = idx[0] == layer
    first = idx[0] == 0
    fetch(own, a_own, a_got, a_w, sems.at[0])
    fetch(own, v_own, v_got, v_w, sems.at[1])
    kv = own_kv[...]
    for r in far_kv:
        kv = kv + r[...].astype(F32)
    half = HK * HD
    qk = jnp.concatenate([dq[...], kv[:, :half]], axis=1)
    qk_in = rot_back(qk, cos[...], sin[...]).astype(BF)
    v_in = kv[:, half:].astype(BF)
    rows, depth = x.shape
    width = (HQ + HK) * HD
    padded = jnp.concatenate([jnp.zeros((rows, HQ * HD), BF), v_in], axis=1)
    arrive(a_own, a_w, sems.at[0])
    arrive(v_own, v_w, sems.at[1])
    ng = nt(qk_in, a_w[:, :width]) + nt(padded, v_w[:, :width])
    z = x[...].astype(F32)
    gain = gain_row(a_w[:, width:])
    inv = norm_scale(z)
    weighted = ng * gain
    part = inv * weighted - z * (inv * inv * inv) * jnp.mean(z * weighted, axis=-1, keepdims=True)
    ig_out[...] = (rg[...] + part).astype(BF)
    nv = normed[...]
    qk_grad = jnp.concatenate([tn(nv, qk_in).astype(BF), gain_tile(ng * z * inv)], axis=1)
    lanes = lax.broadcasted_iota(jnp.int32, (depth, width), 1)
    v_grad = tn(nv, padded).astype(BF)
    ogv = og[...]
    merged = jnp.where(lanes < HQ * HD, ogv[:, :width], v_grad)
    vo_grad = jnp.concatenate([merged, ogv[:, width:]], axis=1)
    m_out[...] = jnp.where(first, qk_grad, vo_grad)
    t_out[...] = jnp.where(first, vo_grad, qk_grad)


def input_back(layer, idx, x, normed, dq, own_kv, far_kv, rg, weights, cos, sin, og):
    rows, depth = x.shape
    a_own, a_got, v_own, v_got = weights
    args = (idx, x, normed, dq, own_kv) + tuple(far_kv)
    args += (rg, a_own, a_got, v_own, v_got, cos, sin, og)
    return call(
        functools.partial(input_back_kernel, layer, len(far_kv)),
        (shape((rows, depth), BF), shape(a_own.shape, BF), shape(a_own.shape, BF)),
        [IN_SMEM] + [IN_VMEM] * (5 + len(far_kv)) + [ANYWHERE] * 4 + [IN_VMEM] * 3,
        [pltpu.VMEM(a_own.shape, BF), pltpu.VMEM(v_own.shape, BF), pltpu.SemaphoreType.DMA((2,))],
        args,
        2 * 2 * rows * depth * 1536,
    )


def crossed(value, axis, mask):
    count = lax.axis_size(axis)
    return lax.ppermute(value, axis, [(i, i ^ mask) for i in range(count)])


def shifted(value, distance):
    devices = range(lax.axis_size("ctx"))
    return lax.ppermute(value, "ctx", [(i, i + distance) for i in devices if i + distance in devices])


def other_core(value):
    return crossed(value, "section", 1)


def bits_of(count):
    return [b for b in range(count.bit_length() - 1)]


def gather_rows(piece, order):
    me = lax.axis_index("fsdp")
    count = lax.axis_size("fsdp")
    have = []
    value = piece
    for bit in order:
        got = crossed(value, "fsdp", 1 << bit)
        low = ((me >> bit) & 1) == 0
        place = sum(1 for b in have if b > bit)
        value = jnp.stack([jnp.where(low, value, got), jnp.where(low, got, value)], axis=place)
        have.append(bit)
    return value.reshape((count * piece.shape[0],) + piece.shape[1:])


def scatter_rows(value, order):
    me = lax.axis_index("fsdp")
    count = lax.axis_size("fsdp")
    bits = len(order)
    rows = value.shape[0] // count
    value = value.reshape((2,) * bits + (rows,) + value.shape[1:])
    left = sorted(order, reverse=True)
    for bit in order:
        mine = (me >> bit) & 1
        place = left.index(bit)
        send = lax.dynamic_index_in_dim(value, 1 - mine, place, keepdims=False)
        keep = lax.dynamic_index_in_dim(value, mine, place, keepdims=False)
        got = crossed(send, "fsdp", 1 << bit)
        value = (keep.astype(F32) + got.astype(F32)).astype(BF)
        left.remove(bit)
    return value


def body(
    inputs,
    positions,
    out_grad,
    attn_gain,
    query_proj,
    key_proj,
    value_proj,
    out_proj,
    mlp_gain,
    gate_proj,
    up_proj,
    down_proj,
):
    core = lax.axis_index("section")
    first = core == 0
    ctx = lax.axis_index("ctx")
    ctx_count = lax.axis_size("ctx")
    fsdp_count = lax.axis_size("fsdp")
    micro, seqs, block, depth = inputs.shape
    shard = query_proj.shape[1]
    rows = seqs * block
    idx = jnp.stack([core, ctx]).astype(jnp.int32)
    up_order = bits_of(fsdp_count)
    down_order = up_order[::-1]

    def pick(a, b):
        return jnp.where(first, a, b)

    def tile_of(gain):
        return jnp.broadcast_to(gain[0][:, None], (shard, LANES))

    a_piece = jnp.concatenate([query_proj[0], key_proj[0], tile_of(attn_gain)], axis=1)
    v_piece = jnp.concatenate([out_proj[0], value_proj[0], tile_of(mlp_gain)], axis=1)
    a_own = gather_rows(a_piece, up_order)
    v_own = gather_rows(v_piece, down_order)
    a_got = other_core(a_own)
    v_got = other_core(v_own)
    attn_w = (a_own, a_got, v_own, v_got)

    half = down_proj.shape[1] // 2
    g_keep = pick(gate_proj[0], up_proj[0])
    g_got = other_core(pick(up_proj[0], gate_proj[0]))
    d_keep = pick(down_proj[0, :half], down_proj[0, half:])
    d_got = other_core(pick(down_proj[0, half:], down_proj[0, :half]))
    g_mine = []
    g_theirs = []
    d_full = []
    for layer in range(2):
        g_piece = pick(g_keep, g_got) if layer == 0 else pick(g_got, g_keep)
        d_piece = pick(d_keep, d_got) if layer == 0 else pick(d_got, d_keep)
        mine = gather_rows(g_piece, up_order)
        g_mine.append(mine)
        g_theirs.append(other_core(mine))
        d_mine = gather_rows(d_piece, down_order).reshape(fsdp_count, half, depth)
        d_other = other_core(d_mine)
        full = jnp.stack([pick(d_mine, d_other), pick(d_other, d_mine)], axis=1)
        d_full.append(full.reshape(2 * fsdp_count * half, depth))

    places = lax.dynamic_index_in_dim(positions, core, 0, keepdims=False).reshape(rows)
    frequency = rope_base ** (-(jnp.arange(HD // 2, dtype=F32) * 2.0 / HD))
    angles = places.astype(F32)[:, None] * frequency
    cos = jnp.concatenate([jnp.cos(angles)] * 4, axis=-1)
    sin = jnp.concatenate([jnp.sin(angles)] * 4, axis=-1)

    x = lax.dynamic_index_in_dim(inputs, core, 0, keepdims=False).reshape(rows, depth)
    saved = []
    for layer in range(2):
        normed, q, kv_own = attn_in(layer, idx, x, attn_w, cos, sin)
        kv = [kv_own] + [shifted(kv_own, d) for d in range(1, ctx_count)]
        attn, lse = attend(idx, q, kv)
        y, resid, mn, gate, up, hid = mlp(
            layer, idx, x, attn, attn_w, g_mine[layer], g_theirs[layer], d_full[layer]
        )
        saved.append((x, normed, q, kv, attn, lse, resid, mn, gate, up, hid))
        x = y
    outs = [saved[1][0], x]

    e = lax.dynamic_index_in_dim(out_grad, core, 0, keepdims=False).reshape(rows, depth)
    entry = [None, None]
    finished = [None, None]
    for layer in (1, 0):
        x, normed, q, kv, attn, lse, resid, mn, gate, up, hid = saved[layer]
        gm, gt, rg, mix, ag, mg = mlp_back(
            layer, idx, e, resid, gate, up, g_mine[layer], g_theirs[layer], d_full[layer], attn_w
        )
        ggm, ggt, dg, og = mlp_grads(hid, e, mn, gm, gt, attn, mix, mg)
        back = attend_back(idx, q, ag, lse, kv)
        dq, own_kv = back[:2]
        far_kv = [shifted(part, -(d + 1)) for d, part in enumerate(back[2:])]
        e, a_mine, a_theirs = input_back(
            layer, idx, x, normed, dq, own_kv, far_kv, rg, attn_w, cos, sin, og
        )
        entry[layer] = e

        def joined(mine, theirs):
            got = other_core(theirs)
            return (mine.astype(F32) + got.astype(F32)).astype(BF)

        g_sum = scatter_rows(joined(ggm, ggt), up_order)
        dg = dg.reshape(fsdp_count, 2, half, depth)
        d_mine = lax.dynamic_index_in_dim(dg, core, 1, keepdims=False)
        d_theirs = lax.dynamic_index_in_dim(dg, 1 - core, 1, keepdims=False)
        d_sum = scatter_rows(joined(d_mine, d_theirs).reshape(fsdp_count * half, depth), down_order)
        a_sum = scatter_rows(joined(a_mine, a_theirs), up_order)
        finished[layer] = tuple(lax.psum(v, "ctx") for v in (g_sum, d_sum, a_sum))

    def own_layer(zero, one):
        keep = pick(zero, one)
        got = other_core(pick(one, zero))
        return (pick(keep, got), pick(got, keep))

    section_out = jnp.stack(own_layer(outs[0], outs[1])).reshape(1, micro, seqs, block, depth)
    input_grad = jnp.stack(own_layer(entry[0], entry[1])).reshape(1, micro, seqs, block, depth)
    gate_g, up_g = own_layer(finished[0][0], finished[1][0])
    down_g = jnp.concatenate(own_layer(finished[0][1], finished[1][1]), axis=0)
    qk_g, ov_g = own_layer(finished[0][2], finished[1][2])
    qw, kw = HQ * HD, HK * HD

    def out(v):
        return v.astype(F32)[None]

    return (
        section_out,
        input_grad,
        out(qk_g[:, qw + kw]),
        out(qk_g[:, :qw]),
        out(qk_g[:, qw : qw + kw]),
        out(ov_g[:, depth : depth + kw]),
        out(ov_g[:, :depth]),
        out(ov_g[:, depth + kw]),
        out(gate_g),
        out(up_g),
        out(down_g),
    )


def solution(mesh):
    rows = P(None, "fsdp", "ctx", None)
    both = P("section", None, "fsdp", "ctx", None)
    vec = P("section", "fsdp")
    mat = P("section", "fsdp", None)
    return jax.shard_map(
        body,
        mesh=mesh,
        in_specs=(rows, P(None, "fsdp", "ctx"), rows, vec, mat, mat, mat, mat, vec, mat, mat, mat),
        out_specs=(both, both, vec, mat, mat, mat, mat, vec, mat, mat, mat),
        check_vma=False,
    )
```

```python
import functools

import jax
import jax.numpy as jnp
from jax import lax
from jax.experimental import pallas as pl
from jax.experimental.pallas import tpu as pltpu
from jax.sharding import PartitionSpec as P

HQ = 9
HK = 3
HD = 64
GROUP = HQ // HK
LANES = 128

epsilon = 1e-05
rope_base = 100000.0
masked_score = -1e30

BF = jnp.bfloat16
F32 = jnp.float32
VMEM_LIMIT = 56 * 1024 * 1024

IN_VMEM = pl.BlockSpec(memory_space=pltpu.VMEM)
IN_SMEM = pl.BlockSpec(memory_space=pltpu.SMEM)
ANYWHERE = pl.BlockSpec(memory_space=pl.ANY)


def nn(a, b):
    return lax.dot_general(a, b, (((1,), (0,)), ((), ())), preferred_element_type=F32)


def nt(a, b):
    return lax.dot_general(a, b, (((1,), (1,)), ((), ())), preferred_element_type=F32)


def tn(a, b):
    return lax.dot_general(a, b, (((0,), (0,)), ((), ())), preferred_element_type=F32)


def shape(dims, kind):
    return jax.ShapeDtypeStruct(dims, kind)


def call(kernel, outs, in_specs, scratch, args, flops, after=()):
    count = len(args)
    late = len(after)
    inner = kernel

    def kernel(*refs):
        inner(*refs[:count], *refs[count + late :])

    in_specs = list(in_specs) + [ANYWHERE] * late
    moved = sum(a.size * a.dtype.itemsize for a in args)
    moved += sum(o.size * o.dtype.itemsize for o in outs)
    return pl.pallas_call(
        kernel,
        out_shape=tuple(outs),
        in_specs=in_specs,
        out_specs=tuple(IN_VMEM for _ in outs),
        scratch_shapes=scratch,
        compiler_params=pltpu.CompilerParams(vmem_limit_bytes=VMEM_LIMIT),
        cost_estimate=pl.CostEstimate(flops=flops // 1000, bytes_accessed=moved // 1000, transcendentals=0),
    )(*args, *after)


def fetch(flag, yes_ref, no_ref, target, sem):
    @pl.when(flag)
    def _():
        pltpu.make_async_copy(yes_ref, target, sem).start()

    @pl.when(jnp.logical_not(flag))
    def _():
        pltpu.make_async_copy(no_ref, target, sem).start()


def arrive(ref, target, sem):
    pltpu.make_async_copy(ref, target, sem).wait()


def fetch_down(parts, core, mine, theirs, target, sem):
    if parts == 0:
        pltpu.make_async_copy(mine, target, sem).start()
        return
    half = mine.shape[0] // parts
    for i in range(parts):
        rows = pl.ds(i * half, half)
        for source, place in ((mine, core), (theirs, 1 - core)):
            start = pl.multiple_of((2 * i + place) * half, half)
            pltpu.make_async_copy(source.at[rows], target.at[pl.ds(start, half)], sem).start()


def arrive_down(target, sem):
    pltpu.make_async_copy(target, target, sem).wait()


def norm_scale(z):
    return lax.rsqrt(jnp.mean(z * z, axis=-1, keepdims=True) + epsilon)


def gain_row(tile):
    lane = lax.broadcasted_iota(jnp.int32, (8, LANES), 1)
    pick = jnp.where(lane == 0, 1.0, 0.0).astype(BF)
    return nt(pick, tile)[0:1]


def gain_tile(rows):
    return tn(rows.astype(BF), jnp.ones((rows.shape[0], LANES), BF)).astype(BF)


def wide(table, width):
    return jnp.concatenate([table] * (width // LANES), axis=1)


def low_half(width, rows):
    lane = lax.broadcasted_iota(jnp.int32, (rows, width), 1)
    return lax.rem(lane, HD) < HD // 2


def rot(a, cosine, sine):
    width = a.shape[1]
    up = pltpu.roll(a, HD // 2, 1)
    down = pltpu.roll(a, width - HD // 2, 1)
    turned = jnp.where(low_half(width, a.shape[0]), -down, up)
    return a * wide(cosine, width) + turned * wide(sine, width)


def rot_back(b, cosine, sine):
    width = b.shape[1]
    c = b * wide(sine, width)
    up = pltpu.roll(c, HD // 2, 1)
    down = pltpu.roll(c, width - HD // 2, 1)
    turned = jnp.where(low_half(width, b.shape[0]), down, -up)
    return b * wide(cosine, width) + turned


def attn_in_kernel(layer, idx, x, a_own, a_got, v_own, v_got, cos, sin, normed_out, q_out, kv_out, a_w, v_w, sems):
    own = idx[0] == layer
    fetch(own, a_own, a_got, a_w, sems.at[0])
    fetch(own, v_own, v_got, v_w, sems.at[1])
    z = x[...].astype(F32)
    scaled = z * norm_scale(z)
    arrive(a_own, a_w, sems.at[0])
    width = (HQ + HK) * HD
    gain = gain_row(a_w[:, width:])
    normed = (scaled * gain).astype(BF)
    normed_out[...] = normed
    qk = rot(nn(normed, a_w[:, :width]), cos[...], sin[...])
    q_out[...] = (qk[:, : HQ * HD].astype(BF).astype(F32) * HD ** (-0.5)).astype(BF)
    arrive(v_own, v_w, sems.at[1])
    value = nn(normed, v_w[:, :width])[:, HQ * HD :]
    kv_out[...] = jnp.concatenate([qk[:, HQ * HD :].astype(BF), value.astype(BF)], axis=1)


def attn_in(layer, idx, x, weights, cos, sin, after=()):
    rows, depth = x.shape
    a_own, a_got, v_own, v_got = weights
    args = (idx, x, a_own, a_got, v_own, v_got, cos, sin)
    return call(
        functools.partial(attn_in_kernel, layer),
        (shape((rows, depth), BF), shape((rows, HQ * HD), BF), shape((rows, 2 * HK * HD), BF)),
        [IN_SMEM, IN_VMEM] + [ANYWHERE] * 4 + [IN_VMEM] * 2,
        [pltpu.VMEM(a_own.shape, BF), pltpu.VMEM(v_own.shape, BF), pltpu.SemaphoreType.DMA((2,))],
        args,
        2 * rows * depth * 1536,
        after,
    )


def score_block(keys, query, block, reach, causal):
    s = nt(keys, query)
    if block == 0:
        return jnp.where(causal, s, masked_score)
    return jnp.where(block <= reach, s, masked_score)


def causal_mask(rows):
    key_at = lax.broadcasted_iota(jnp.int32, (rows, rows), 0)
    query_at = lax.broadcasted_iota(jnp.int32, (rows, rows), 1)
    return key_at <= query_at


def head(values, at):
    return values[:, at * HD : (at + 1) * HD]


def attend_kernel(blocks, idx, q, *refs):
    kv = [r[...] for r in refs[:blocks]]
    attn_out, lse_out = refs[blocks:]
    rows = q.shape[0]
    reach = idx[1]
    causal = causal_mask(rows)
    queries = q[...]
    pieces = []
    lse_out[...] = jnp.zeros_like(lse_out)
    for g in range(HK):
        keys = [head(b, g) for b in kv]
        values = jnp.concatenate([head(b, HK + g) for b in kv], axis=0)
        for i in range(GROUP):
            h = g * GROUP + i
            query = head(queries, h)
            s = jnp.concatenate(
                [score_block(k, query, d, reach, causal) for d, k in enumerate(keys)], axis=0
            )
            top = jnp.max(s, axis=0, keepdims=True)
            p = jnp.exp(s - top)
            total = jnp.sum(p, axis=0, keepdims=True)
            lse_out[h : h + 1, :] = top + jnp.log(total)
            p_low = (p * (1.0 / total)).astype(BF)
            pieces.append(tn(p_low, values).astype(BF))
    attn_out[...] = jnp.concatenate(pieces, axis=1)


def attend(idx, q, kv, after=()):
    rows = q.shape[0]
    return call(
        functools.partial(attend_kernel, len(kv)),
        (shape((rows, HQ * HD), BF), shape((16, rows), F32)),
        [IN_SMEM] + [IN_VMEM] * (1 + len(kv)),
        [],
        (idx, q) + tuple(kv),
        2 * 2 * rows * rows * len(kv) * HQ * HD * 4,
        after,
    )


def mlp_kernel(layer, parts, idx, x, attn, v_own, v_got, g_m, g_t, d_m, d_t, y_out, resid_out, mn_out, gate_out, up_out, hid_out, v_w, d_w, sems):
    own = idx[0] == layer
    first = idx[0] == 0
    fetch(own, v_own, v_got, v_w, sems.at[0])
    fetch_down(parts, idx[0], d_m, d_t, d_w, sems.at[1])
    arrive(v_own, v_w, sems.at[0])
    width = HQ * HD
    depth = x.shape[1]
    resid = x[...].astype(F32) + nn(attn[...], v_w[:, :depth])
    resid_out[...] = resid
    gain = gain_row(v_w[:, width + HK * HD :])
    mn = (resid * norm_scale(resid) * gain).astype(BF)
    mn_out[...] = mn
    mine = nn(mn, g_m[...])
    theirs = nn(mn, g_t[...])
    gate = jnp.where(first, mine, theirs)
    up = jnp.where(first, theirs, mine)
    gate_out[...] = gate
    up_out[...] = up
    hid = (gate * jax.nn.sigmoid(gate) * up).astype(BF)
    hid_out[...] = hid
    arrive_down(d_w, sems.at[1])
    y_out[...] = (resid + nn(hid, d_w[:, :depth])).astype(BF)


def mlp(layer, parts, idx, x, attn, weights, g_m, g_t, d_m, d_t, after=()):
    rows, depth = x.shape
    _, _, v_own, v_got = weights
    ff = g_m.shape[1]
    args = (idx, x, attn, v_own, v_got, g_m, g_t, d_m, d_t)
    return call(
        functools.partial(mlp_kernel, layer, parts),
        (
            shape((rows, depth), BF),
            shape((rows, depth), F32),
            shape((rows, depth), BF),
            shape((rows, ff), F32),
            shape((rows, ff), F32),
            shape((rows, ff), BF),
        ),
        [IN_SMEM, IN_VMEM, IN_VMEM] + [ANYWHERE] * 2 + [IN_VMEM] * 2 + [ANYWHERE] * 2,
        [
            pltpu.VMEM(v_own.shape, BF),
            pltpu.VMEM((ff, d_m.shape[1]), BF),
            pltpu.SemaphoreType.DMA((2,)),
        ],
        args,
        2 * rows * depth * (3 * ff + depth),
        after,
    )


def mlp_back_kernel(layer, parts, idx, e, resid, gate, up, g_m, g_t, d_m, d_t, v_own, v_got, gm_out, gt_out, rg_out, mix_out, ag_out, mg_out, v_w, d_w, sems):
    own = idx[0] == layer
    first = idx[0] == 0
    fetch_down(parts, idx[0], d_m, d_t, d_w, sems.at[1])
    fetch(own, v_own, v_got, v_w, sems.at[0])
    low = e[...]
    arrive_down(d_w, sems.at[1])
    hg = nt(low, d_w[:, : e.shape[1]])
    gv = gate[...]
    sig = jax.nn.sigmoid(gv)
    g_in = (hg * up[...] * sig * (1.0 + gv * (1.0 - sig))).astype(BF)
    u_in = (hg * gv * sig).astype(BF)
    mine = jnp.where(first, g_in, u_in)
    theirs = jnp.where(first, u_in, g_in)
    gm_out[...] = mine
    gt_out[...] = theirs
    ng = nt(mine, g_m[...]) + nt(theirs, g_t[...])
    arrive(v_own, v_w, sems.at[0])
    width = HQ * HD
    depth = e.shape[1]
    gain = gain_row(v_w[:, width + HK * HD :])
    z = resid[...]
    inv = norm_scale(z)
    weighted = ng * gain
    mg_out[...] = gain_tile(ng * z * inv)
    part = inv * weighted - z * (inv * inv * inv) * jnp.mean(z * weighted, axis=-1, keepdims=True)
    rg = low.astype(F32) + part
    rg_out[...] = rg
    mix = rg.astype(BF)
    mix_out[...] = mix
    ag_out[...] = nt(mix, v_w[:, :depth]).astype(BF)


def mlp_back(layer, parts, idx, e, resid, gate, up, g_m, g_t, d_m, d_t, weights, after=()):
    rows, depth = e.shape
    _, _, v_own, v_got = weights
    ff = g_m.shape[1]
    args = (idx, e, resid, gate, up, g_m, g_t, d_m, d_t, v_own, v_got)
    return call(
        functools.partial(mlp_back_kernel, layer, parts),
        (
            shape((rows, ff), BF),
            shape((rows, ff), BF),
            shape((rows, depth), F32),
            shape((rows, depth), BF),
            shape((rows, HQ * HD), BF),
            shape((depth, LANES), BF),
        ),
        [IN_SMEM] + [IN_VMEM] * 6 + [ANYWHERE] * 4,
        [
            pltpu.VMEM(v_own.shape, BF),
            pltpu.VMEM((ff, d_m.shape[1]), BF),
            pltpu.SemaphoreType.DMA((2,)),
        ],
        args,
        2 * rows * depth * (3 * ff + depth),
        after,
    )


def padded_rows(count, step=16):
    return count + -count % step


class Packing:
    def __init__(self, shard, half, ff, depth):
        self.shard = shard
        self.half = half
        self.shard_step = padded_rows(shard)
        self.half_step = padded_rows(half)
        self.gate_tiles = ff // LANES
        self.down_tiles = padded_rows(depth, LANES) // LANES
        self.out_tiles = (self.down_tiles + 1) // 2
        self.down_at = self.gate_tiles * self.shard_step
        self.out_at = self.down_at + self.down_tiles * self.half_step
        used = self.out_at + self.out_tiles * self.shard_step
        self.used = used
        self.rows = self.down_at + padded_rows(used - self.down_at, 64)
        self.entry_tiles = (HQ + 2 * HK + 1) * HD // LANES // 2
        self.entry_rows = self.entry_tiles * self.shard_step


def tile(value, at):
    return value[:, at * LANES : (at + 1) * LANES]


def mlp_grads_kernel(pack, idx, hid, e, mn, gm, gt, attn, mix, mg, m_out, t_out):
    parts = m_out.shape[0]
    first = idx[0] == 0
    depth = mn.shape[1]
    shard, half = pack.shard, pack.half
    mnv = mn[...]
    fill = pack.down_tiles * LANES - depth
    down = tn(hid[...], e[...]).astype(BF)
    down = jnp.concatenate([down, jnp.zeros((down.shape[0], fill), BF)], axis=1)
    outward = tn(attn[...], mix[...]).astype(BF)
    outward = jnp.concatenate([outward, mg[:, :fill]], axis=1)
    blank = jnp.zeros((shard, LANES), BF)
    for out, side, low in ((m_out, gm, first), (t_out, gt, jnp.logical_not(first))):
        gate = tn(mnv, side[...]).astype(BF)
        for f in range(parts):
            rows = slice(f * shard, (f + 1) * shard)
            for k in range(pack.gate_tiles):
                at = k * pack.shard_step
                out[f, at : at + shard, :] = tile(gate[rows], k)
            low_half = down[2 * f * half : (2 * f + 1) * half]
            high_half = down[(2 * f + 1) * half : (2 * f + 2) * half]
            own_half = jnp.where(low, low_half, high_half)
            for k in range(pack.down_tiles):
                at = pack.down_at + k * pack.half_step
                out[f, at : at + half, :] = tile(own_half, k)
            for k in range(pack.out_tiles):
                at = pack.out_at + k * pack.shard_step
                other = k + pack.out_tiles
                high = tile(outward[rows], other) if other < pack.down_tiles else blank
                out[f, at : at + shard, :] = jnp.where(low, tile(outward[rows], k), high)
            if pack.used < pack.rows:
                out[f, pack.used :, :] = jnp.zeros((pack.rows - pack.used, LANES), BF)


def mlp_grads(pack, parts, idx, hid, e, mn, gm, gt, attn, mix, mg, after=()):
    rows, depth = e.shape
    ff = gm.shape[1]
    return call(
        functools.partial(mlp_grads_kernel, pack),
        (shape((parts, pack.rows, LANES), BF), shape((parts, pack.rows, LANES), BF)),
        [IN_SMEM] + [IN_VMEM] * 8,
        [],
        (idx, hid, e, mn, gm, gt, attn, mix, mg),
        2 * rows * depth * (3 * ff + depth),
        after,
    )


def halves(idx, zero, one, got):
    first = idx[0] == 0
    keep = jnp.where(first, zero[...], one[...])
    other = got[...]
    return jnp.where(first, keep, other), jnp.where(first, other, keep)


def unpack_mlp_kernel(pack, idx, zero, one, got, gate_out, up_out, down_out, o_out, gain_out):
    shard, half = pack.shard, pack.half
    both = halves(idx, zero, one, got)
    for value, out in zip(both, (gate_out, up_out)):
        for k in range(pack.gate_tiles):
            at = k * pack.shard_step
            out[:, k * LANES : (k + 1) * LANES] = value[at : at + shard].astype(F32)
    depth = down_out.shape[1]
    for side, value in enumerate(both):
        tiles = []
        for k in range(pack.down_tiles):
            at = pack.down_at + k * pack.half_step
            tiles.append(value[at : at + half])
        wide_rows = jnp.concatenate(tiles, axis=1)[:, :depth]
        down_out[side * half : (side + 1) * half, :] = wide_rows.astype(F32)
    tiles = []
    for k in range(pack.down_tiles):
        at = pack.out_at + (k % pack.out_tiles) * pack.shard_step
        tiles.append(both[k // pack.out_tiles][at : at + shard])
    o_out[...] = jnp.concatenate(tiles, axis=1)[:, :depth].astype(F32)
    gain_out[...] = tiles[-1].astype(F32)


def unpack_mlp(pack, idx, zero, one, got, ff, depth):
    return call(
        functools.partial(unpack_mlp_kernel, pack),
        (
            shape((pack.shard, ff), F32),
            shape((pack.shard, ff), F32),
            shape((2 * pack.half, depth), F32),
            shape((pack.shard, depth), F32),
            shape((pack.shard, LANES), F32),
        ),
        [IN_SMEM] + [IN_VMEM] * 3,
        [],
        (idx, zero, one, got),
        1000,
    )


def unpack_entry_kernel(pack, idx, zero, one, got, q_out, k_out, v_out, gain_out):
    shard = pack.shard
    tiles = []
    for value in halves(idx, zero, one, got):
        for k in range(pack.entry_tiles):
            at = k * pack.shard_step
            tiles.append(value[at : at + shard])
    full = jnp.concatenate(tiles, axis=1).astype(F32)
    qw, kw = HQ * HD, HK * HD
    q_out[...] = full[:, :qw]
    k_out[...] = full[:, qw : qw + kw]
    v_out[...] = full[:, qw + kw : qw + 2 * kw]
    gain_out[...] = tiles[-1].astype(F32)


def unpack_entry(pack, idx, zero, one, got):
    qw, kw = HQ * HD, HK * HD
    return call(
        functools.partial(unpack_entry_kernel, pack),
        (
            shape((pack.shard, qw), F32),
            shape((pack.shard, kw), F32),
            shape((pack.shard, kw), F32),
            shape((pack.shard, LANES), F32),
        ),
        [IN_SMEM] + [IN_VMEM] * 3,
        [],
        (idx, zero, one, got),
        1000,
    )


def attend_back_kernel(blocks, idx, q, ag, lse, *refs):
    kv = [r[...] for r in refs[:blocks]]
    dq_out, own_out = refs[blocks : blocks + 2]
    far_out = refs[blocks + 2 :]
    rows = q.shape[0]
    reach = idx[1]
    causal = causal_mask(rows)
    queries = q[...]
    grads = ag[...]
    dq_parts = []
    dk_parts = []
    dv_parts = []
    for g in range(HK):
        keys = [head(b, g) for b in kv]
        all_keys = jnp.concatenate(keys, axis=0)
        values = jnp.concatenate([head(b, HK + g) for b in kv], axis=0)
        dk = None
        dv = None
        for i in range(GROUP):
            h = g * GROUP + i
            query = head(queries, h)
            grad = head(grads, h)
            s = jnp.concatenate(
                [score_block(k, query, d, reach, causal) for d, k in enumerate(keys)], axis=0
            )
            p = jnp.exp(s - lse[h : h + 1, :])
            dp = nt(values, grad)
            delta = jnp.sum(p * dp, axis=0, keepdims=True)
            ds = (p * (dp - delta)).astype(BF)
            dv_h = nn(p.astype(BF), grad)
            dk_h = nn(ds, query)
            dk = dk_h if dk is None else dk + dk_h
            dv = dv_h if dv is None else dv + dv_h
            dq_parts.append(tn(ds, all_keys) * HD ** (-0.5))
        dk_parts.append(dk)
        dv_parts.append(dv)
    dq_out[...] = jnp.concatenate(dq_parts, axis=1)
    joined = jnp.concatenate(dk_parts + dv_parts, axis=1)
    own_out[...] = joined[:rows]
    for d, out in enumerate(far_out):
        out[...] = joined[(d + 1) * rows : (d + 2) * rows].astype(BF)


def attend_back(idx, q, ag, lse, kv, after=()):
    rows = q.shape[0]
    outs = [shape((rows, HQ * HD), F32), shape((rows, 2 * HK * HD), F32)]
    outs += [shape((rows, 2 * HK * HD), BF) for _ in kv[1:]]
    return call(
        functools.partial(attend_back_kernel, len(kv)),
        outs,
        [IN_SMEM] + [IN_VMEM] * (3 + len(kv)),
        [],
        (idx, q, ag, lse) + tuple(kv),
        5 * 2 * rows * rows * len(kv) * HQ * HD * 4,
        after,
    )


def input_back_kernel(layer, pack, far, idx, x, normed, dq, own_kv, *refs):
    far_kv = refs[:far]
    rg, a_own, a_got, v_own, v_got, cos, sin, ig_out, m_out, t_out, a_w, v_w, sems = refs[far:]
    own = idx[0] == layer
    first = idx[0] == 0
    fetch(own, a_own, a_got, a_w, sems.at[0])
    fetch(own, v_own, v_got, v_w, sems.at[1])
    kv = own_kv[...]
    for r in far_kv:
        kv = kv + r[...].astype(F32)
    half = HK * HD
    qk = jnp.concatenate([dq[...], kv[:, :half]], axis=1)
    qk_in = rot_back(qk, cos[...], sin[...]).astype(BF)
    v_in = kv[:, half:].astype(BF)
    rows, depth = x.shape
    width = (HQ + HK) * HD
    padded = jnp.concatenate([jnp.zeros((rows, HQ * HD), BF), v_in], axis=1)
    arrive(a_own, a_w, sems.at[0])
    arrive(v_own, v_w, sems.at[1])
    ng = nt(qk_in, a_w[:, :width]) + nt(padded, v_w[:, :width])
    z = x[...].astype(F32)
    gain = gain_row(a_w[:, width:])
    inv = norm_scale(z)
    weighted = ng * gain
    part = inv * weighted - z * (inv * inv * inv) * jnp.mean(z * weighted, axis=-1, keepdims=True)
    ig_out[...] = (rg[...] + part).astype(BF)
    nv = normed[...]
    grads = jnp.concatenate(
        [
            tn(nv, qk_in).astype(BF),
            tn(nv, v_in).astype(BF),
            gain_tile(ng * z * inv)[:, :HD],
        ],
        axis=1,
    )
    shard = pack.shard
    for f in range(m_out.shape[0]):
        piece = grads[f * shard : (f + 1) * shard]
        for k in range(pack.entry_tiles):
            at = k * pack.shard_step
            low = tile(piece, k)
            high = tile(piece, k + pack.entry_tiles)
            m_out[f, at : at + shard, :] = jnp.where(first, low, high)
            t_out[f, at : at + shard, :] = jnp.where(first, high, low)


def input_back(layer, pack, parts, idx, x, normed, dq, own_kv, far_kv, rg, weights, cos, sin, after=()):
    rows, depth = x.shape
    a_own, a_got, v_own, v_got = weights
    args = (idx, x, normed, dq, own_kv) + tuple(far_kv)
    args += (rg, a_own, a_got, v_own, v_got, cos, sin)
    packed = (parts, pack.entry_rows, LANES)
    return call(
        functools.partial(input_back_kernel, layer, pack, len(far_kv)),
        (shape((rows, depth), BF), shape(packed, BF), shape(packed, BF)),
        [IN_SMEM] + [IN_VMEM] * (5 + len(far_kv)) + [ANYWHERE] * 4 + [IN_VMEM] * 2,
        [pltpu.VMEM(a_own.shape, BF), pltpu.VMEM(v_own.shape, BF), pltpu.SemaphoreType.DMA((2,))],
        args,
        2 * 2 * rows * depth * 1536,
        after,
    )


def crossed(value, axis, mask):
    count = lax.axis_size(axis)
    return lax.ppermute(value, axis, [(i, i ^ mask) for i in range(count)])


def shifted(value, distance):
    devices = range(lax.axis_size("ctx"))
    return lax.ppermute(value, "ctx", [(i, i + distance) for i in devices if i + distance in devices])


def other_core(value):
    return crossed(value, "section", 1)


def bits_of(count):
    return [b for b in range(count.bit_length() - 1)]


def held(value, *deps):
    return lax.optimization_barrier((value,) + deps)[0]


def gather_step(value, have, bit, wait):
    me = lax.axis_index("fsdp")
    got = crossed(value, "fsdp", 1 << bit)
    if wait:
        got = held(got, *wait)
    low = ((me >> bit) & 1) == 0
    place = sum(1 for b in have if b > bit)
    return jnp.stack([jnp.where(low, value, got), jnp.where(low, got, value)], axis=place)


def gather_some(values, orders, first, last, wait=()):
    for step in range(first, last):
        late = wait if step == last - 1 else ()
        values = [gather_step(v, o[:step], o[step], late) for v, o in zip(values, orders)]
    return values


def whole_rows(value):
    return value.reshape((value.size // value.shape[-1],) + value.shape[-1:])


def cut(value, left, bit):
    mine = (lax.axis_index("fsdp") >> bit) & 1
    place = sorted(left, reverse=True).index(bit)
    send = lax.dynamic_index_in_dim(value, 1 - mine, place, keepdims=False)
    keep = lax.dynamic_index_in_dim(value, mine, place, keepdims=False)
    return send, keep


def added(halves, bit, wait=()):
    send, keep = halves
    got = crossed(send, "fsdp", 1 << bit)
    if wait:
        got = held(got, *wait)
    return (keep.astype(F32) + got.astype(F32)).astype(BF)


def first_cut(value, order):
    count = lax.axis_size("fsdp")
    value = value.reshape((2,) * len(order) + (value.shape[0] // count,) + value.shape[1:])
    return cut(value, order, order[0])


def scatter_rest(value, order, wait=()):
    for step in range(1, len(order)):
        late = wait if step == len(order) - 1 else ()
        value = added(cut(value, order[step:], order[step]), order[step], late)
    return value


def sum_over_ctx(value):
    count = lax.axis_size("ctx")
    if count & (count - 1):
        return lax.psum(value, "ctx")
    for bit in bits_of(count):
        value = (value.astype(F32) + crossed(value, "ctx", 1 << bit).astype(F32)).astype(BF)
    return value


def ctx_begin(value, wait=()):
    me = lax.axis_index("ctx") & 1
    size = value.shape[0] // 2
    send = lax.dynamic_slice_in_dim(value, (1 - me) * size, size, 0)
    keep = lax.dynamic_slice_in_dim(value, me * size, size, 0)
    got = crossed(send, "ctx", 1)
    if wait:
        got = held(got, *wait)
    return (keep.astype(F32) + got.astype(F32)).astype(BF)


def ctx_middle(value, wait=()):
    for bit in bits_of(lax.axis_size("ctx"))[1:]:
        value = added_over_ctx(value, bit, wait)
    return value


def ctx_end(value, wait=()):
    low = (lax.axis_index("ctx") & 1) == 0
    got = crossed(value, "ctx", 1)
    if wait:
        got = held(got, *wait)
    return jnp.concatenate([jnp.where(low, value, got), jnp.where(low, got, value)], axis=0)


def added_over_ctx(value, bit, wait):
    got = crossed(value, "ctx", 1 << bit)
    if wait:
        got = held(got, *wait)
    return (value.astype(F32) + got.astype(F32)).astype(BF)


def body(
    inputs,
    positions,
    out_grad,
    attn_gain,
    query_proj,
    key_proj,
    value_proj,
    out_proj,
    mlp_gain,
    gate_proj,
    up_proj,
    down_proj,
):
    core = lax.axis_index("section")
    first = core == 0
    ctx = lax.axis_index("ctx")
    ctx_count = lax.axis_size("ctx")
    fsdp_count = lax.axis_size("fsdp")
    micro, seqs, block, depth = inputs.shape
    shard = query_proj.shape[1]
    rows = seqs * block
    idx = jnp.stack([core, ctx]).astype(jnp.int32)
    up_order = bits_of(fsdp_count)
    down_order = up_order[::-1]

    def pick(a, b):
        return jnp.where(first, a, b)

    def tile_of(gain):
        return jnp.broadcast_to(gain[0][:, None], (shard, LANES))

    a_piece = jnp.concatenate([query_proj[0], key_proj[0], tile_of(attn_gain)], axis=1)
    v_piece = jnp.concatenate([out_proj[0], value_proj[0], tile_of(mlp_gain)], axis=1)
    steps = len(up_order)
    a_own, v_own = gather_some([a_piece, v_piece], [up_order, down_order], 0, steps)
    a_own = whole_rows(a_own)
    v_own = whole_rows(v_own)
    a_got = other_core(a_own)
    v_got = other_core(v_own)
    attn_w = (a_own, a_got, v_own, v_got)

    half = down_proj.shape[1] // 2
    g_keep = pick(gate_proj[0], up_proj[0])
    g_got = other_core(pick(up_proj[0], gate_proj[0]))
    wide_down = jnp.pad(down_proj[0], ((0, 0), (0, -depth % LANES)))
    d_keep = pick(wide_down[:half], wide_down[half:])
    d_got = other_core(pick(wide_down[half:], wide_down[:half]))
    def feed_forward_pieces(layer):
        g_piece = pick(g_keep, g_got) if layer == 0 else pick(g_got, g_keep)
        d_piece = pick(d_keep, d_got) if layer == 0 else pick(d_got, d_keep)
        return [g_piece, d_piece]

    parts_of_down = fsdp_count if half % 16 == 0 else 0

    def down_halves(mine, theirs):
        if parts_of_down:
            return (mine, theirs)
        mine, theirs = [v.reshape(fsdp_count, half, -1) for v in (mine, theirs)]
        full = jnp.stack([pick(mine, theirs), pick(theirs, mine)], axis=1)
        full = whole_rows(full)
        return (full, full)

    places = lax.dynamic_index_in_dim(positions, core, 0, keepdims=False).reshape(rows)
    frequency = rope_base ** (-(jnp.arange(HD // 2, dtype=F32) * 2.0 / HD))
    angles = places.astype(F32)[:, None] * frequency
    cos = jnp.concatenate([jnp.cos(angles)] * 4, axis=-1)
    sin = jnp.concatenate([jnp.sin(angles)] * 4, axis=-1)

    x = lax.dynamic_index_in_dim(inputs, core, 0, keepdims=False).reshape(rows, depth)
    saved = []
    ff_w = [None, None]
    for layer in range(2):
        normed, q, kv_own = attn_in(layer, idx, x, attn_w, cos, sin)
        kv = [kv_own] + [shifted(kv_own, d) for d in range(1, ctx_count)]
        orders = [up_order, down_order] if layer == 0 else [down_order, up_order]
        if layer == 0:
            parts = lax.optimization_barrier(tuple(feed_forward_pieces(0)) + (a_own, v_own))[:2]
        parts = gather_some(parts, orders, 0, 1, (normed,))
        if layer == 1:
            parts = lax.optimization_barrier(tuple(parts) + (normed,))[:2]
        g_all, d_all = gather_some(parts, orders, 1, steps)
        attn, lse = attend(idx, q, kv)
        g_all, d_all, attn = lax.optimization_barrier((whole_rows(g_all), whole_rows(d_all), attn))
        ff_w[layer] = (g_all, other_core(g_all)) + down_halves(d_all, other_core(d_all))
        if layer == 0:
            parts = lax.optimization_barrier(tuple(feed_forward_pieces(1)) + (g_all, d_all))[:2]
        y, resid, mn, gate, up, hid = mlp(layer, parts_of_down, idx, x, attn, attn_w, *ff_w[layer])
        saved.append((x, normed, q, kv, attn, lse, resid, mn, gate, up, hid))
        x = y
    outs = [saved[1][0], x]

    pack = Packing(shard, half, gate_proj.shape[2], depth)

    def joined(mine, theirs):
        got = other_core(theirs)
        return (mine.astype(F32) + got.astype(F32)).astype(BF)

    e = lax.dynamic_index_in_dim(out_grad, core, 0, keepdims=False).reshape(rows, depth)
    entry = [None, None]
    def feed_forward_back(layer, e, after, between):
        x, normed, q, kv, attn, lse, resid, mn, gate, up, hid = saved[layer]
        gm, gt, rg, mix, ag, mg = mlp_back(
            layer, parts_of_down, idx, e, resid, gate, up, *ff_w[layer], attn_w, after
        )
        done = between(ag) if between else ()
        first = tuple(d[0] if isinstance(d, tuple) else d for d in done)
        mine, theirs = mlp_grads(pack, fsdp_count, idx, hid, e, mn, gm, gt, attn, mix, mg, first)
        result = (rg, ag, joined(mine, theirs))
        return result + (done,) if between else result

    def attention_back(layer, ag, after):
        x, normed, q, kv, attn, lse, resid, mn, gate, up, hid = saved[layer]
        back = attend_back(idx, q, ag, lse, kv, after)
        far_kv = [shifted(part, -(d + 1)) for d, part in enumerate(back[2:])]
        return back[0], back[1], far_kv

    def entry_back(layer, dq, own_kv, far_kv, rg, after):
        x, normed = saved[layer][:2]
        e, mine, theirs = input_back(
            layer, pack, fsdp_count, idx, x, normed, dq, own_kv, far_kv, rg, attn_w, cos, sin, after
        )
        entry[layer] = e
        return e, joined(mine, theirs)

    orders = (up_order, down_order)

    def start(value, at):
        return [first_cut(value[:, :at], up_order), first_cut(value[:, at:], down_order)]

    def sends(cuts):
        return tuple(c[0] for c in cuts)

    def first_sums(cuts, wait):
        return [added(c, o[0], wait) for c, o in zip(cuts, orders)]

    def last_sums(values, wait):
        values = [scatter_rest(v, o, wait) for v, o in zip(values, orders)]
        return jnp.concatenate(values, axis=1)[0]

    middle = pack.down_at
    entry_middle = pack.entry_rows // 2
    rg, ag, m1 = feed_forward_back(1, e, (), ())
    m1 = start(m1, middle)
    dq, own_kv, far_kv = attention_back(1, ag, sends(m1))
    e, a1 = entry_back(1, dq, own_kv, far_kv, rg, ())
    m1 = first_sums(m1, (e,))

    def between(ag):
        return (last_sums(m1, (ag,)), *start(a1, entry_middle))

    rg, ag, m0, m1 = feed_forward_back(0, e, tuple(m1), between)
    m0 = start(m0, middle)
    m1, a1 = m1[0], list(m1[1:])
    m1 = ctx_begin(m1, (m0[0][0],))
    a1 = first_sums(a1, (m0[0][0],))
    dq, own_kv, far_kv = attention_back(0, ag, sends(m0) + tuple(a1) + (m1,))
    a1 = last_sums(a1, (dq,))
    m0 = first_sums(m0, (dq,))
    m1 = ctx_middle(m1, (far_kv[-1],))
    e, a0 = entry_back(0, dq, own_kv, far_kv, rg, (a1, m1) + tuple(m0))
    a0 = start(a0, entry_middle)
    late = sends(a0)[0]
    m0 = jnp.concatenate([last_sums(m0, (e,)), a1], axis=0)
    m0 = ctx_begin(m0, (late,))
    a0 = first_sums(a0, ())
    m1 = ctx_end(m1, tuple(a0))
    a0 = last_sums(a0, ())
    m0 = ctx_end(ctx_middle(m0, (a0,)))
    a0 = sum_over_ctx(a0)
    m0, a1 = m0[: pack.rows], m0[pack.rows :]

    def own_layer(zero, one):
        keep = pick(zero, one)
        got = other_core(pick(one, zero))
        return (pick(keep, got), pick(got, keep))

    outs[0], outs[1], entry[0], entry[1], _ = lax.optimization_barrier(
        (outs[0], outs[1], entry[0], entry[1], late)
    )
    section_out = jnp.stack(own_layer(outs[0], outs[1])).reshape(1, micro, seqs, block, depth)
    input_grad = jnp.stack(own_layer(entry[0], entry[1])).reshape(1, micro, seqs, block, depth)
    ff = gate_proj.shape[2]
    m_got = other_core(pick(m1, m0))
    gate_g, up_g, down_g, out_g, mlp_gain_g = unpack_mlp(pack, idx, m0, m1, m_got, ff, depth)
    a_got = other_core(pick(a1, a0))
    query_g, key_g, value_g, attn_gain_g = unpack_entry(pack, idx, a0, a1, a_got)
    spare = LANES - HD

    return (
        section_out,
        input_grad,
        attn_gain_g[:, spare][None],
        query_g[None],
        key_g[None],
        value_g[None],
        out_g[None],
        mlp_gain_g[:, spare][None],
        gate_g[None],
        up_g[None],
        down_g[None],
    )


def solution(mesh):
    rows = P(None, "fsdp", "ctx", None)
    both = P("section", None, "fsdp", "ctx", None)
    vec = P("section", "fsdp")
    mat = P("section", "fsdp", None)
    return jax.shard_map(
        body,
        mesh=mesh,
        in_specs=(rows, P(None, "fsdp", "ctx"), rows, vec, mat, mat, mat, mat, vec, mat, mat, mat),
        out_specs=(both, both, vec, mat, mat, mat, mat, vec, mat, mat, mat),
        check_vma=False,
    )
```

```python
import functools

import jax
import jax.numpy as jnp
from jax import lax
from jax.experimental import pallas as pl
from jax.experimental.pallas import tpu as pltpu
from jax.sharding import PartitionSpec as P

HQ = 9
HK = 3
HD = 64
GROUP = HQ // HK
LANES = 128

epsilon = 1e-05
rope_base = 100000.0
masked_score = -1e30

BF = jnp.bfloat16
F32 = jnp.float32
MIB = 1024 * 1024

IN_VMEM = pl.BlockSpec(memory_space=pltpu.VMEM)
IN_SMEM = pl.BlockSpec(memory_space=pltpu.SMEM)
ANYWHERE = pl.BlockSpec(memory_space=pl.ANY)


def nn(a, b):
    return lax.dot_general(a, b, (((1,), (0,)), ((), ())), preferred_element_type=F32)


def nt(a, b):
    return lax.dot_general(a, b, (((1,), (1,)), ((), ())), preferred_element_type=F32)


def tn(a, b):
    return lax.dot_general(a, b, (((0,), (0,)), ((), ())), preferred_element_type=F32)


def shape(dims, kind):
    return jax.ShapeDtypeStruct(dims, kind)


def call(kernel, outs, in_specs, scratch, args, flops, after=(), limit=56):
    count = len(args)
    late = len(after)
    inner = kernel

    def kernel(*refs):
        inner(*refs[:count], *refs[count + late :])

    in_specs = list(in_specs) + [ANYWHERE] * late
    moved = sum(a.size * a.dtype.itemsize for a in args)
    moved += sum(o.size * o.dtype.itemsize for o in outs)
    return pl.pallas_call(
        kernel,
        out_shape=tuple(outs),
        in_specs=in_specs,
        out_specs=tuple(IN_VMEM for _ in outs),
        scratch_shapes=scratch,
        compiler_params=pltpu.CompilerParams(vmem_limit_bytes=limit * MIB),
        cost_estimate=pl.CostEstimate(flops=flops // 1000, bytes_accessed=moved // 1000, transcendentals=0),
    )(*args, *after)


def fetch(flag, yes_ref, no_ref, target, sem):
    @pl.when(flag)
    def _():
        pltpu.make_async_copy(yes_ref, target, sem).start()

    @pl.when(jnp.logical_not(flag))
    def _():
        pltpu.make_async_copy(no_ref, target, sem).start()


def arrive(ref, target, sem):
    pltpu.make_async_copy(ref, target, sem).wait()


def fetch_down(parts, core, mine, theirs, target, sem):
    if parts == 0:
        pltpu.make_async_copy(mine, target, sem).start()
        return
    half = mine.shape[0] // parts
    for i in range(parts):
        rows = pl.ds(i * half, half)
        for source, place in ((mine, core), (theirs, 1 - core)):
            start = pl.multiple_of((2 * i + place) * half, half)
            pltpu.make_async_copy(source.at[rows], target.at[pl.ds(start, half)], sem).start()


def arrive_down(target, sem):
    pltpu.make_async_copy(target, target, sem).wait()


def norm_scale(z):
    return lax.rsqrt(jnp.mean(z * z, axis=-1, keepdims=True) + epsilon)


def gain_row(tile):
    lane = lax.broadcasted_iota(jnp.int32, (8, LANES), 1)
    pick = jnp.where(lane == 0, 1.0, 0.0).astype(BF)
    return nt(pick, tile)[0:1]


def gain_tile(rows):
    return tn(rows.astype(BF), jnp.ones((rows.shape[0], LANES), BF)).astype(BF)


def wide(table, width):
    return jnp.concatenate([table] * (width // LANES), axis=1)


def low_half(width, rows):
    lane = lax.broadcasted_iota(jnp.int32, (rows, width), 1)
    return lax.rem(lane, HD) < HD // 2


def rot(a, cosine, sine):
    width = a.shape[1]
    up = pltpu.roll(a, HD // 2, 1)
    down = pltpu.roll(a, width - HD // 2, 1)
    turned = jnp.where(low_half(width, a.shape[0]), -down, up)
    return a * wide(cosine, width) + turned * wide(sine, width)


def rot_back(b, cosine, sine):
    width = b.shape[1]
    c = b * wide(sine, width)
    up = pltpu.roll(c, HD // 2, 1)
    down = pltpu.roll(c, width - HD // 2, 1)
    turned = jnp.where(low_half(width, b.shape[0]), down, -up)
    return b * wide(cosine, width) + turned


def attn_in_kernel(layer, idx, x, a_own, a_got, v_own, v_got, cos, sin, normed_out, q_out, kv_out, a_w, v_w, sems):
    own = idx[0] == layer
    fetch(own, a_own, a_got, a_w, sems.at[0])
    fetch(own, v_own, v_got, v_w, sems.at[1])
    z = x[...].astype(F32)
    scaled = z * norm_scale(z)
    arrive(a_own, a_w, sems.at[0])
    width = (HQ + HK) * HD
    gain = gain_row(a_w[:, width:])
    normed = (scaled * gain).astype(BF)
    normed_out[...] = normed
    qk = rot(nn(normed, a_w[:, :width]), cos[...], sin[...])
    q_out[...] = (qk[:, : HQ * HD].astype(BF).astype(F32) * HD ** (-0.5)).astype(BF)
    arrive(v_own, v_w, sems.at[1])
    value = nn(normed, v_w[:, :width])[:, HQ * HD :]
    kv_out[...] = jnp.concatenate([qk[:, HQ * HD :].astype(BF), value.astype(BF)], axis=1)


def attn_in(layer, idx, x, weights, cos, sin, after=()):
    rows, depth = x.shape
    a_own, a_got, v_own, v_got = weights
    args = (idx, x, a_own, a_got, v_own, v_got, cos, sin)
    return call(
        functools.partial(attn_in_kernel, layer),
        (shape((rows, depth), BF), shape((rows, HQ * HD), BF), shape((rows, 2 * HK * HD), BF)),
        [IN_SMEM, IN_VMEM] + [ANYWHERE] * 4 + [IN_VMEM] * 2,
        [pltpu.VMEM(a_own.shape, BF), pltpu.VMEM(v_own.shape, BF), pltpu.SemaphoreType.DMA((2,))],
        args,
        2 * rows * depth * 1536,
        after,
        limit=40,
    )


def score_block(keys, query, block, reach, causal):
    s = nt(keys, query)
    if block == 0:
        return jnp.where(causal, s, masked_score)
    return jnp.where(block <= reach, s, masked_score)


def causal_mask(rows):
    key_at = lax.broadcasted_iota(jnp.int32, (rows, rows), 0)
    query_at = lax.broadcasted_iota(jnp.int32, (rows, rows), 1)
    return key_at <= query_at


def head(values, at):
    return values[:, at * HD : (at + 1) * HD]


def attend_kernel(blocks, idx, q, *refs):
    kv = [r[...] for r in refs[:blocks]]
    attn_out, lse_out = refs[blocks:]
    rows = q.shape[0]
    reach = idx[1]
    causal = causal_mask(rows)
    queries = q[...]
    pieces = []
    lse_out[...] = jnp.zeros_like(lse_out)
    for g in range(HK):
        keys = [head(b, g) for b in kv]
        values = jnp.concatenate([head(b, HK + g) for b in kv], axis=0)
        for i in range(GROUP):
            h = g * GROUP + i
            query = head(queries, h)
            s = jnp.concatenate(
                [score_block(k, query, d, reach, causal) for d, k in enumerate(keys)], axis=0
            )
            top = jnp.max(s, axis=0, keepdims=True)
            p = jnp.exp(s - top)
            total = jnp.sum(p, axis=0, keepdims=True)
            lse_out[h : h + 1, :] = top + jnp.log(total)
            p_low = (p * (1.0 / total)).astype(BF)
            pieces.append(tn(p_low, values).astype(BF))
    attn_out[...] = jnp.concatenate(pieces, axis=1)


def attend(idx, q, kv, after=()):
    rows = q.shape[0]
    return call(
        functools.partial(attend_kernel, len(kv)),
        (shape((rows, HQ * HD), BF), shape((16, rows), F32)),
        [IN_SMEM] + [IN_VMEM] * (1 + len(kv)),
        [],
        (idx, q) + tuple(kv),
        2 * 2 * rows * rows * len(kv) * HQ * HD * 4,
        after,
        limit=40,
    )


def mlp_kernel(layer, parts, idx, x, attn, v_own, v_got, g_m, g_t, d_m, d_t, y_out, resid_out, mn_out, gate_out, up_out, hid_out, v_w, d_w, sems):
    own = idx[0] == layer
    first = idx[0] == 0
    fetch(own, v_own, v_got, v_w, sems.at[0])
    fetch_down(parts, idx[0], d_m, d_t, d_w, sems.at[1])
    arrive(v_own, v_w, sems.at[0])
    width = HQ * HD
    depth = x.shape[1]
    resid = x[...].astype(F32) + nn(attn[...], v_w[:, :depth])
    resid_out[...] = resid
    gain = gain_row(v_w[:, width + HK * HD :])
    mn = (resid * norm_scale(resid) * gain).astype(BF)
    mn_out[...] = mn
    mine = nn(mn, g_m[...])
    theirs = nn(mn, g_t[...])
    gate = jnp.where(first, mine, theirs)
    up = jnp.where(first, theirs, mine)
    gate_out[...] = gate
    up_out[...] = up
    hid = (gate * jax.nn.sigmoid(gate) * up).astype(BF)
    hid_out[...] = hid
    arrive_down(d_w, sems.at[1])
    y_out[...] = (resid + nn(hid, d_w[:, :depth])).astype(BF)


def mlp(layer, parts, idx, x, attn, weights, g_m, g_t, d_m, d_t, after=()):
    rows, depth = x.shape
    _, _, v_own, v_got = weights
    ff = g_m.shape[1]
    args = (idx, x, attn, v_own, v_got, g_m, g_t, d_m, d_t)
    return call(
        functools.partial(mlp_kernel, layer, parts),
        (
            shape((rows, depth), BF),
            shape((rows, depth), F32),
            shape((rows, depth), BF),
            shape((rows, ff), F32),
            shape((rows, ff), F32),
            shape((rows, ff), BF),
        ),
        [IN_SMEM, IN_VMEM, IN_VMEM] + [ANYWHERE] * 2 + [IN_VMEM] * 2 + [ANYWHERE] * 2,
        [
            pltpu.VMEM(v_own.shape, BF),
            pltpu.VMEM((ff, d_m.shape[1]), BF),
            pltpu.SemaphoreType.DMA((2,)),
        ],
        args,
        2 * rows * depth * (3 * ff + depth),
        after,
        limit=40,
    )


def mlp_back_kernel(layer, parts, idx, e, resid, gate, up, g_m, g_t, d_m, d_t, v_own, v_got, gm_out, gt_out, rg_out, mix_out, ag_out, mg_out, v_w, d_w, sems):
    own = idx[0] == layer
    first = idx[0] == 0
    fetch_down(parts, idx[0], d_m, d_t, d_w, sems.at[1])
    fetch(own, v_own, v_got, v_w, sems.at[0])
    low = e[...]
    arrive_down(d_w, sems.at[1])
    hg = nt(low, d_w[:, : e.shape[1]])
    gv = gate[...]
    sig = jax.nn.sigmoid(gv)
    g_in = (hg * up[...] * sig * (1.0 + gv * (1.0 - sig))).astype(BF)
    u_in = (hg * gv * sig).astype(BF)
    mine = jnp.where(first, g_in, u_in)
    theirs = jnp.where(first, u_in, g_in)
    gm_out[...] = mine
    gt_out[...] = theirs
    ng = nt(mine, g_m[...]) + nt(theirs, g_t[...])
    arrive(v_own, v_w, sems.at[0])
    width = HQ * HD
    depth = e.shape[1]
    gain = gain_row(v_w[:, width + HK * HD :])
    z = resid[...]
    inv = norm_scale(z)
    weighted = ng * gain
    mg_out[...] = gain_tile(ng * z * inv)
    part = inv * weighted - z * (inv * inv * inv) * jnp.mean(z * weighted, axis=-1, keepdims=True)
    rg = low.astype(F32) + part
    rg_out[...] = rg
    mix = rg.astype(BF)
    mix_out[...] = mix
    ag_out[...] = nt(mix, v_w[:, :depth]).astype(BF)


def mlp_back(layer, parts, idx, e, resid, gate, up, g_m, g_t, d_m, d_t, weights, after=()):
    rows, depth = e.shape
    _, _, v_own, v_got = weights
    ff = g_m.shape[1]
    args = (idx, e, resid, gate, up, g_m, g_t, d_m, d_t, v_own, v_got)
    return call(
        functools.partial(mlp_back_kernel, layer, parts),
        (
            shape((rows, ff), BF),
            shape((rows, ff), BF),
            shape((rows, depth), F32),
            shape((rows, depth), BF),
            shape((rows, HQ * HD), BF),
            shape((depth, LANES), BF),
        ),
        [IN_SMEM] + [IN_VMEM] * 6 + [ANYWHERE] * 4,
        [
            pltpu.VMEM(v_own.shape, BF),
            pltpu.VMEM((ff, d_m.shape[1]), BF),
            pltpu.SemaphoreType.DMA((2,)),
        ],
        args,
        2 * rows * depth * (3 * ff + depth),
        after,
        limit=40,
    )


def padded_rows(count, step=16):
    return count + -count % step


class Packing:
    def __init__(self, shard, half, ff, depth):
        self.shard = shard
        self.half = half
        self.shard_step = padded_rows(shard)
        self.half_step = padded_rows(half)
        self.gate_tiles = ff // LANES
        self.down_tiles = padded_rows(depth, LANES) // LANES
        self.out_tiles = (self.down_tiles + 1) // 2
        self.down_at = self.gate_tiles * self.shard_step
        self.out_at = self.down_at + self.down_tiles * self.half_step
        used = self.out_at + self.out_tiles * self.shard_step
        self.used = used
        self.rows = self.down_at + padded_rows(used - self.down_at, 64)
        self.entry_tiles = (HQ + 2 * HK + 1) * HD // LANES // 2
        self.entry_rows = self.entry_tiles * self.shard_step


def tile(value, at):
    return value[:, at * LANES : (at + 1) * LANES]


def mlp_grads_kernel(pack, idx, hid, e, mn, gm, gt, attn, mix, mg, m_out, t_out):
    parts = m_out.shape[0]
    first = idx[0] == 0
    depth = mn.shape[1]
    shard, half = pack.shard, pack.half
    mnv = mn[...]
    fill = pack.down_tiles * LANES - depth
    down = tn(hid[...], e[...]).astype(BF)
    down = jnp.concatenate([down, jnp.zeros((down.shape[0], fill), BF)], axis=1)
    outward = tn(attn[...], mix[...]).astype(BF)
    outward = jnp.concatenate([outward, mg[:, :fill]], axis=1)
    blank = jnp.zeros((shard, LANES), BF)
    for out, side, low in ((m_out, gm, first), (t_out, gt, jnp.logical_not(first))):
        gate = tn(mnv, side[...]).astype(BF)
        for f in range(parts):
            rows = slice(f * shard, (f + 1) * shard)
            for k in range(pack.gate_tiles):
                at = k * pack.shard_step
                out[f, at : at + shard, :] = tile(gate[rows], k)
            low_half = down[2 * f * half : (2 * f + 1) * half]
            high_half = down[(2 * f + 1) * half : (2 * f + 2) * half]
            own_half = jnp.where(low, low_half, high_half)
            for k in range(pack.down_tiles):
                at = pack.down_at + k * pack.half_step
                out[f, at : at + half, :] = tile(own_half, k)
            for k in range(pack.out_tiles):
                at = pack.out_at + k * pack.shard_step
                other = k + pack.out_tiles
                high = tile(outward[rows], other) if other < pack.down_tiles else blank
                out[f, at : at + shard, :] = jnp.where(low, tile(outward[rows], k), high)
            if pack.used < pack.rows:
                out[f, pack.used :, :] = jnp.zeros((pack.rows - pack.used, LANES), BF)


def mlp_grads(pack, parts, idx, hid, e, mn, gm, gt, attn, mix, mg, after=()):
    rows, depth = e.shape
    ff = gm.shape[1]
    return call(
        functools.partial(mlp_grads_kernel, pack),
        (shape((parts, pack.rows, LANES), BF), shape((parts, pack.rows, LANES), BF)),
        [IN_SMEM] + [IN_VMEM] * 8,
        [],
        (idx, hid, e, mn, gm, gt, attn, mix, mg),
        2 * rows * depth * (3 * ff + depth),
        after,
        limit=40,
    )


def halves(idx, zero, one, got):
    first = idx[0] == 0
    keep = jnp.where(first, zero[...], one[...])
    other = got[...]
    return jnp.where(first, keep, other), jnp.where(first, other, keep)


def unpack_mlp_kernel(pack, idx, zero, one, got, gate_out, up_out, down_out, o_out, gain_out):
    shard, half = pack.shard, pack.half
    both = halves(idx, zero, one, got)
    for value, out in zip(both, (gate_out, up_out)):
        for k in range(pack.gate_tiles):
            at = k * pack.shard_step
            out[:, k * LANES : (k + 1) * LANES] = value[at : at + shard].astype(F32)
    depth = down_out.shape[1]
    for side, value in enumerate(both):
        tiles = []
        for k in range(pack.down_tiles):
            at = pack.down_at + k * pack.half_step
            tiles.append(value[at : at + half])
        wide_rows = jnp.concatenate(tiles, axis=1)[:, :depth]
        down_out[side * half : (side + 1) * half, :] = wide_rows.astype(F32)
    tiles = []
    for k in range(pack.down_tiles):
        at = pack.out_at + (k % pack.out_tiles) * pack.shard_step
        tiles.append(both[k // pack.out_tiles][at : at + shard])
    o_out[...] = jnp.concatenate(tiles, axis=1)[:, :depth].astype(F32)
    gain_out[...] = tiles[-1].astype(F32)


def unpack_mlp(pack, idx, zero, one, got, ff, depth):
    return call(
        functools.partial(unpack_mlp_kernel, pack),
        (
            shape((pack.shard, ff), F32),
            shape((pack.shard, ff), F32),
            shape((2 * pack.half, depth), F32),
            shape((pack.shard, depth), F32),
            shape((pack.shard, LANES), F32),
        ),
        [IN_SMEM] + [IN_VMEM] * 3,
        [],
        (idx, zero, one, got),
        1000,
    )


def unpack_entry_kernel(pack, idx, zero, one, got, q_out, k_out, v_out, gain_out):
    shard = pack.shard
    tiles = []
    for value in halves(idx, zero, one, got):
        for k in range(pack.entry_tiles):
            at = k * pack.shard_step
            tiles.append(value[at : at + shard])
    full = jnp.concatenate(tiles, axis=1).astype(F32)
    qw, kw = HQ * HD, HK * HD
    q_out[...] = full[:, :qw]
    k_out[...] = full[:, qw : qw + kw]
    v_out[...] = full[:, qw + kw : qw + 2 * kw]
    gain_out[...] = tiles[-1].astype(F32)


def unpack_entry(pack, idx, zero, one, got):
    qw, kw = HQ * HD, HK * HD
    return call(
        functools.partial(unpack_entry_kernel, pack),
        (
            shape((pack.shard, qw), F32),
            shape((pack.shard, kw), F32),
            shape((pack.shard, kw), F32),
            shape((pack.shard, LANES), F32),
        ),
        [IN_SMEM] + [IN_VMEM] * 3,
        [],
        (idx, zero, one, got),
        1000,
    )


def attend_back_kernel(blocks, idx, q, ag, lse, *refs):
    kv = [r[...] for r in refs[:blocks]]
    dq_out, own_out = refs[blocks : blocks + 2]
    far_out = refs[blocks + 2 :]
    rows = q.shape[0]
    reach = idx[1]
    causal = causal_mask(rows)
    queries = q[...]
    grads = ag[...]
    dq_parts = []
    dk_parts = []
    dv_parts = []
    for g in range(HK):
        keys = [head(b, g) for b in kv]
        all_keys = jnp.concatenate(keys, axis=0)
        values = jnp.concatenate([head(b, HK + g) for b in kv], axis=0)
        dk = None
        dv = None
        for i in range(GROUP):
            h = g * GROUP + i
            query = head(queries, h)
            grad = head(grads, h)
            s = jnp.concatenate(
                [score_block(k, query, d, reach, causal) for d, k in enumerate(keys)], axis=0
            )
            p = jnp.exp(s - lse[h : h + 1, :])
            dp = nt(values, grad)
            delta = jnp.sum(p * dp, axis=0, keepdims=True)
            ds = (p * (dp - delta)).astype(BF)
            dv_h = nn(p.astype(BF), grad)
            dk_h = nn(ds, query)
            dk = dk_h if dk is None else dk + dk_h
            dv = dv_h if dv is None else dv + dv_h
            dq_parts.append(tn(ds, all_keys) * HD ** (-0.5))
        dk_parts.append(dk)
        dv_parts.append(dv)
    dq_out[...] = jnp.concatenate(dq_parts, axis=1)
    joined = jnp.concatenate(dk_parts + dv_parts, axis=1)
    own_out[...] = joined[:rows]
    for d, out in enumerate(far_out):
        out[...] = joined[(d + 1) * rows : (d + 2) * rows].astype(BF)


def attend_back(idx, q, ag, lse, kv, after=()):
    rows = q.shape[0]
    outs = [shape((rows, HQ * HD), F32), shape((rows, 2 * HK * HD), F32)]
    outs += [shape((rows, 2 * HK * HD), BF) for _ in kv[1:]]
    return call(
        functools.partial(attend_back_kernel, len(kv)),
        outs,
        [IN_SMEM] + [IN_VMEM] * (3 + len(kv)),
        [],
        (idx, q, ag, lse) + tuple(kv),
        5 * 2 * rows * rows * len(kv) * HQ * HD * 4,
        after,
    )


def input_back_kernel(layer, pack, far, idx, x, normed, dq, own_kv, *refs):
    far_kv = refs[:far]
    rg, a_own, a_got, v_own, v_got, cos, sin, ig_out, m_out, t_out, a_w, v_w, sems = refs[far:]
    own = idx[0] == layer
    first = idx[0] == 0
    fetch(own, a_own, a_got, a_w, sems.at[0])
    fetch(own, v_own, v_got, v_w, sems.at[1])
    kv = own_kv[...]
    for r in far_kv:
        kv = kv + r[...].astype(F32)
    half = HK * HD
    qk = jnp.concatenate([dq[...], kv[:, :half]], axis=1)
    qk_in = rot_back(qk, cos[...], sin[...]).astype(BF)
    v_in = kv[:, half:].astype(BF)
    rows, depth = x.shape
    width = (HQ + HK) * HD
    padded = jnp.concatenate([jnp.zeros((rows, HQ * HD), BF), v_in], axis=1)
    arrive(a_own, a_w, sems.at[0])
    arrive(v_own, v_w, sems.at[1])
    ng = nt(qk_in, a_w[:, :width]) + nt(padded, v_w[:, :width])
    z = x[...].astype(F32)
    gain = gain_row(a_w[:, width:])
    inv = norm_scale(z)
    weighted = ng * gain
    part = inv * weighted - z * (inv * inv * inv) * jnp.mean(z * weighted, axis=-1, keepdims=True)
    ig_out[...] = (rg[...] + part).astype(BF)
    nv = normed[...]
    grads = jnp.concatenate(
        [
            tn(nv, qk_in).astype(BF),
            tn(nv, v_in).astype(BF),
            gain_tile(ng * z * inv)[:, :HD],
        ],
        axis=1,
    )
    shard = pack.shard
    for f in range(m_out.shape[0]):
        piece = grads[f * shard : (f + 1) * shard]
        for k in range(pack.entry_tiles):
            at = k * pack.shard_step
            low = tile(piece, k)
            high = tile(piece, k + pack.entry_tiles)
            m_out[f, at : at + shard, :] = jnp.where(first, low, high)
            t_out[f, at : at + shard, :] = jnp.where(first, high, low)


def input_back(layer, pack, parts, idx, x, normed, dq, own_kv, far_kv, rg, weights, cos, sin, after=()):
    rows, depth = x.shape
    a_own, a_got, v_own, v_got = weights
    args = (idx, x, normed, dq, own_kv) + tuple(far_kv)
    args += (rg, a_own, a_got, v_own, v_got, cos, sin)
    packed = (parts, pack.entry_rows, LANES)
    return call(
        functools.partial(input_back_kernel, layer, pack, len(far_kv)),
        (shape((rows, depth), BF), shape(packed, BF), shape(packed, BF)),
        [IN_SMEM] + [IN_VMEM] * (5 + len(far_kv)) + [ANYWHERE] * 4 + [IN_VMEM] * 2,
        [pltpu.VMEM(a_own.shape, BF), pltpu.VMEM(v_own.shape, BF), pltpu.SemaphoreType.DMA((2,))],
        args,
        2 * 2 * rows * depth * 1536,
        after,
    )


def crossed(value, axis, mask):
    count = lax.axis_size(axis)
    return lax.ppermute(value, axis, [(i, i ^ mask) for i in range(count)])


def shifted(value, distance):
    devices = range(lax.axis_size("ctx"))
    return lax.ppermute(value, "ctx", [(i, i + distance) for i in devices if i + distance in devices])


def other_core(value):
    return crossed(value, "section", 1)


def bits_of(count):
    return [b for b in range(count.bit_length() - 1)]


def held(value, *deps):
    return lax.optimization_barrier((value,) + deps)[0]


def gather_step(value, have, bit, wait):
    me = lax.axis_index("fsdp")
    got = crossed(value, "fsdp", 1 << bit)
    if wait:
        got = held(got, *wait)
    low = ((me >> bit) & 1) == 0
    place = sum(1 for b in have if b > bit)
    return jnp.stack([jnp.where(low, value, got), jnp.where(low, got, value)], axis=place)


def gather_some(values, orders, first, last, wait=()):
    for step in range(first, last):
        late = wait if step == last - 1 else ()
        values = [gather_step(v, o[:step], o[step], late) for v, o in zip(values, orders)]
    return values


def whole_rows(value):
    return value.reshape((value.size // value.shape[-1],) + value.shape[-1:])


def cut(value, left, bit):
    mine = (lax.axis_index("fsdp") >> bit) & 1
    place = sorted(left, reverse=True).index(bit)
    send = lax.dynamic_index_in_dim(value, 1 - mine, place, keepdims=False)
    keep = lax.dynamic_index_in_dim(value, mine, place, keepdims=False)
    return send, keep


def added(halves, bit, wait=()):
    send, keep = halves
    got = crossed(send, "fsdp", 1 << bit)
    if wait:
        got = held(got, *wait)
    return (keep.astype(F32) + got.astype(F32)).astype(BF)


def first_cut(value, order):
    count = lax.axis_size("fsdp")
    value = value.reshape((2,) * len(order) + (value.shape[0] // count,) + value.shape[1:])
    return cut(value, order, order[0])


def scatter_rest(value, order, wait=()):
    for step in range(1, len(order)):
        late = wait if step == len(order) - 1 else ()
        value = added(cut(value, order[step:], order[step]), order[step], late)
    return value


def sum_over_ctx(value):
    count = lax.axis_size("ctx")
    if count & (count - 1):
        return lax.psum(value, "ctx")
    for bit in bits_of(count):
        value = (value.astype(F32) + crossed(value, "ctx", 1 << bit).astype(F32)).astype(BF)
    return value


def ctx_cut(value):
    me = lax.axis_index("ctx") & 1
    size = value.shape[0] // 2
    send = lax.dynamic_slice_in_dim(value, (1 - me) * size, size, 0)
    keep = lax.dynamic_slice_in_dim(value, me * size, size, 0)
    return send, keep


def ctx_begin(halves, wait=()):
    send, keep = halves
    got = crossed(send, "ctx", 1)
    if wait:
        got = held(got, *wait)
    return (keep.astype(F32) + got.astype(F32)).astype(BF)


def ctx_middle(value, wait=()):
    for bit in bits_of(lax.axis_size("ctx"))[1:]:
        value = added_over_ctx(value, bit, wait)
    return value


def ctx_end(value, wait=()):
    low = (lax.axis_index("ctx") & 1) == 0
    got = crossed(value, "ctx", 1)
    if wait:
        got = held(got, *wait)
    return jnp.concatenate([jnp.where(low, value, got), jnp.where(low, got, value)], axis=0)


def added_over_ctx(value, bit, wait):
    got = crossed(value, "ctx", 1 << bit)
    if wait:
        got = held(got, *wait)
    return (value.astype(F32) + got.astype(F32)).astype(BF)


def body(
    inputs,
    positions,
    out_grad,
    attn_gain,
    query_proj,
    key_proj,
    value_proj,
    out_proj,
    mlp_gain,
    gate_proj,
    up_proj,
    down_proj,
):
    core = lax.axis_index("section")
    first = core == 0
    ctx = lax.axis_index("ctx")
    ctx_count = lax.axis_size("ctx")
    fsdp_count = lax.axis_size("fsdp")
    micro, seqs, block, depth = inputs.shape
    shard = query_proj.shape[1]
    rows = seqs * block
    idx = jnp.stack([core, ctx]).astype(jnp.int32)
    up_order = bits_of(fsdp_count)
    down_order = up_order[::-1]

    def pick(a, b):
        return jnp.where(first, a, b)

    def tile_of(gain):
        return jnp.broadcast_to(gain[0][:, None], (shard, LANES))

    a_piece = jnp.concatenate([query_proj[0], key_proj[0], tile_of(attn_gain)], axis=1)
    v_piece = jnp.concatenate([out_proj[0], value_proj[0], tile_of(mlp_gain)], axis=1)
    steps = len(up_order)
    a_own, v_own = gather_some([a_piece, v_piece], [up_order, down_order], 0, steps)
    a_own = whole_rows(a_own)
    v_own = whole_rows(v_own)
    a_got = other_core(a_own)
    v_got = other_core(v_own)
    attn_w = (a_own, a_got, v_own, v_got)

    half = down_proj.shape[1] // 2
    g_keep = pick(gate_proj[0], up_proj[0])
    g_got = other_core(pick(up_proj[0], gate_proj[0]))
    wide_down = jnp.pad(down_proj[0], ((0, 0), (0, -depth % LANES)))
    d_keep = pick(wide_down[:half], wide_down[half:])
    d_got = other_core(pick(wide_down[half:], wide_down[:half]))
    def feed_forward_pieces(layer):
        g_piece = pick(g_keep, g_got) if layer == 0 else pick(g_got, g_keep)
        d_piece = pick(d_keep, d_got) if layer == 0 else pick(d_got, d_keep)
        return [g_piece, d_piece]

    parts_of_down = fsdp_count if half % 16 == 0 else 0

    def down_halves(mine, theirs):
        if parts_of_down:
            return (mine, theirs)
        mine, theirs = [v.reshape(fsdp_count, half, -1) for v in (mine, theirs)]
        full = jnp.stack([pick(mine, theirs), pick(theirs, mine)], axis=1)
        full = whole_rows(full)
        return (full, full)

    places = lax.dynamic_index_in_dim(positions, core, 0, keepdims=False).reshape(rows)
    frequency = rope_base ** (-(jnp.arange(HD // 2, dtype=F32) * 2.0 / HD))
    angles = places.astype(F32)[:, None] * frequency
    cos = jnp.concatenate([jnp.cos(angles)] * 4, axis=-1)
    sin = jnp.concatenate([jnp.sin(angles)] * 4, axis=-1)

    x = lax.dynamic_index_in_dim(inputs, core, 0, keepdims=False).reshape(rows, depth)
    saved = []
    ff_w = [None, None]
    for layer in range(2):
        normed, q, kv_own = attn_in(layer, idx, x, attn_w, cos, sin)
        kv = [kv_own] + [shifted(kv_own, d) for d in range(1, ctx_count)]
        orders = [up_order, down_order] if layer == 0 else [down_order, up_order]
        if layer == 0:
            parts = lax.optimization_barrier(tuple(feed_forward_pieces(0)) + (a_own, v_own))[:2]
        parts = gather_some(parts, orders, 0, 1, (normed,))
        if layer == 1:
            parts = lax.optimization_barrier(tuple(parts) + (normed,))[:2]
        g_all, d_all = gather_some(parts, orders, 1, steps)
        attn, lse = attend(idx, q, kv)
        g_all, d_all, attn = lax.optimization_barrier((whole_rows(g_all), whole_rows(d_all), attn))
        ff_w[layer] = (g_all, other_core(g_all)) + down_halves(d_all, other_core(d_all))
        if layer == 0:
            parts = lax.optimization_barrier(tuple(feed_forward_pieces(1)) + (g_all, d_all))[:2]
        y, resid, mn, gate, up, hid = mlp(layer, parts_of_down, idx, x, attn, attn_w, *ff_w[layer])
        saved.append((x, normed, q, kv, attn, lse, resid, mn, gate, up, hid))
        x = y
    outs = [saved[1][0], x]

    pack = Packing(shard, half, gate_proj.shape[2], depth)

    def joined(mine, theirs, wait=()):
        got = other_core(theirs)
        if wait:
            got = held(got, *wait)
        return (mine.astype(F32) + got.astype(F32)).astype(BF)

    e = lax.dynamic_index_in_dim(out_grad, core, 0, keepdims=False).reshape(rows, depth)
    entry = [None, None]
    def feed_forward_back(layer, e, after, between):
        x, normed, q, kv, attn, lse, resid, mn, gate, up, hid = saved[layer]
        gm, gt, rg, mix, ag, mg = mlp_back(
            layer, parts_of_down, idx, e, resid, gate, up, *ff_w[layer], attn_w, after
        )
        done = tuple(between(ag)) if between else ()
        mine, theirs = mlp_grads(pack, fsdp_count, idx, hid, e, mn, gm, gt, attn, mix, mg, done)
        return rg, ag, mine, theirs

    def attention_back(layer, ag, after):
        x, normed, q, kv, attn, lse, resid, mn, gate, up, hid = saved[layer]
        back = attend_back(idx, q, ag, lse, kv, after)
        far_kv = [shifted(part, -(d + 1)) for d, part in enumerate(back[2:])]
        return back[0], back[1], far_kv

    def entry_back(layer, dq, own_kv, far_kv, rg, after):
        x, normed = saved[layer][:2]
        e, mine, theirs = input_back(
            layer, pack, fsdp_count, idx, x, normed, dq, own_kv, far_kv, rg, attn_w, cos, sin, after
        )
        entry[layer] = e
        return e, mine, theirs

    orders = (up_order, down_order)

    def start(value, at):
        return [first_cut(value[:, :at], up_order), first_cut(value[:, at:], down_order)]

    def sends(cuts):
        return tuple(c[0] for c in cuts)

    def first_sums(cuts, wait):
        return [added(c, o[0], wait) for c, o in zip(cuts, orders)]

    def last_sums(values, wait):
        values = [scatter_rest(v, o, wait) for v, o in zip(values, orders)]
        return jnp.concatenate(values, axis=1)[0]

    def next_cuts(values):
        return [cut(v, o[1:], o[1]) for v, o in zip(values, orders)] if steps > 1 else [values]

    middle = pack.down_at
    entry_middle = pack.entry_rows // 2
    rg, ag, mine, theirs = feed_forward_back(1, e, (), None)
    dq, own_kv, far_kv = attention_back(1, ag, (mine,))
    m1 = start(joined(mine, theirs, (dq,)), middle)
    e, a_mine, a_theirs = entry_back(1, dq, own_kv, far_kv, rg, sends(m1))
    m1 = first_sums(m1, (e,))

    def between(ag):
        m1_cut.extend(ctx_cut(last_sums(m1, (ag,))))
        return m1_cut[:1]

    m1_cut = []
    rg, ag, mine, theirs = feed_forward_back(0, e, tuple(m1), between)
    m0 = start(joined(mine, theirs), middle)
    m1 = ctx_begin(m1_cut, (m0[0][0],))
    dq, own_kv, far_kv = attention_back(0, ag, sends(m0) + (m1,))
    a1 = start(joined(a_mine, a_theirs, (dq,)), entry_middle)
    m0 = first_sums(m0, (dq,))
    m1 = ctx_middle(m1, (far_kv[-1],))
    e, a_mine, a_theirs = entry_back(
        0, dq, own_kv, far_kv, rg, sends(next_cuts(m0)) + sends(a1) + (m1,)
    )
    a0 = start(joined(a_mine, a_theirs), entry_middle)
    late = sends(a0)[0]
    m0 = ctx_cut(last_sums(m0, (late,)))
    a1 = first_sums(a1, (m0[0],))
    a0 = first_sums(a0, (m0[0],))
    m0 = ctx_begin(m0, tuple(a0))
    a1 = last_sums(a1, (m0,))
    a0 = last_sums(a0, (m0,))
    m1 = ctx_end(m1, (a0,))
    a0 = sum_over_ctx(jnp.concatenate([a0, a1], axis=0))
    m0 = ctx_end(ctx_middle(m0))
    a0, a1 = a0[: pack.entry_rows], a0[pack.entry_rows :]

    def own_layer(zero, one):
        keep = pick(zero, one)
        got = other_core(pick(one, zero))
        return (pick(keep, got), pick(got, keep))

    outs[0], outs[1], entry[0], entry[1], _ = lax.optimization_barrier(
        (outs[0], outs[1], entry[0], entry[1], late)
    )
    section_out = jnp.stack(own_layer(outs[0], outs[1])).reshape(1, micro, seqs, block, depth)
    input_grad = jnp.stack(own_layer(entry[0], entry[1])).reshape(1, micro, seqs, block, depth)
    ff = gate_proj.shape[2]
    m_got = other_core(pick(m1, m0))
    gate_g, up_g, down_g, out_g, mlp_gain_g = unpack_mlp(pack, idx, m0, m1, m_got, ff, depth)
    a_got = other_core(pick(a1, a0))
    query_g, key_g, value_g, attn_gain_g = unpack_entry(pack, idx, a0, a1, a_got)
    spare = LANES - HD

    return (
        section_out,
        input_grad,
        attn_gain_g[:, spare][None],
        query_g[None],
        key_g[None],
        value_g[None],
        out_g[None],
        mlp_gain_g[:, spare][None],
        gate_g[None],
        up_g[None],
        down_g[None],
    )


def solution(mesh):
    rows = P(None, "fsdp", "ctx", None)
    both = P("section", None, "fsdp", "ctx", None)
    vec = P("section", "fsdp")
    mat = P("section", "fsdp", None)
    return jax.shard_map(
        body,
        mesh=mesh,
        in_specs=(rows, P(None, "fsdp", "ctx"), rows, vec, mat, mat, mat, mat, vec, mat, mat, mat),
        out_specs=(both, both, vec, mat, mat, mat, mat, vec, mat, mat, mat),
        check_vma=False,
    )
```

```python
import functools

import jax
import jax.numpy as jnp
from jax import lax
from jax.experimental import pallas as pl
from jax.experimental.pallas import tpu as pltpu
from jax.sharding import PartitionSpec as P

HQ = 9
HK = 3
HD = 64
GROUP = HQ // HK
LANES = 128

epsilon = 1e-05
rope_base = 100000.0
masked_score = -1e30

BF = jnp.bfloat16
F32 = jnp.float32
MIB = 1024 * 1024

IN_VMEM = pl.BlockSpec(memory_space=pltpu.VMEM)
IN_SMEM = pl.BlockSpec(memory_space=pltpu.SMEM)
ANYWHERE = pl.BlockSpec(memory_space=pl.ANY)


def nn(a, b):
    return lax.dot_general(a, b, (((1,), (0,)), ((), ())), preferred_element_type=F32)


def nt(a, b):
    return lax.dot_general(a, b, (((1,), (1,)), ((), ())), preferred_element_type=F32)


def tn(a, b):
    return lax.dot_general(a, b, (((0,), (0,)), ((), ())), preferred_element_type=F32)


def shape(dims, kind):
    return jax.ShapeDtypeStruct(dims, kind)


def call(kernel, outs, in_specs, scratch, args, flops, after=(), limit=56):
    count = len(args)
    late = len(after)
    inner = kernel

    def kernel(*refs):
        inner(*refs[:count], *refs[count + late :])

    in_specs = list(in_specs) + [ANYWHERE] * late
    moved = sum(a.size * a.dtype.itemsize for a in args)
    moved += sum(o.size * o.dtype.itemsize for o in outs)
    return pl.pallas_call(
        kernel,
        out_shape=tuple(outs),
        in_specs=in_specs,
        out_specs=tuple(IN_VMEM for _ in outs),
        scratch_shapes=scratch,
        compiler_params=pltpu.CompilerParams(vmem_limit_bytes=limit * MIB),
        cost_estimate=pl.CostEstimate(flops=flops // 1000, bytes_accessed=moved // 1000, transcendentals=0),
    )(*args, *after)


def fetch(flag, yes_ref, no_ref, target, sem):
    @pl.when(flag)
    def _():
        pltpu.make_async_copy(yes_ref, target, sem).start()

    @pl.when(jnp.logical_not(flag))
    def _():
        pltpu.make_async_copy(no_ref, target, sem).start()


def arrive(ref, target, sem):
    pltpu.make_async_copy(ref, target, sem).wait()


def fetch_down(parts, core, mine, theirs, target, sem):
    if parts == 0:
        pltpu.make_async_copy(mine, target, sem).start()
        return
    half = mine.shape[0] // parts
    for i in range(parts):
        rows = pl.ds(i * half, half)
        for source, place in ((mine, core), (theirs, 1 - core)):
            start = pl.multiple_of((2 * i + place) * half, half)
            pltpu.make_async_copy(source.at[rows], target.at[pl.ds(start, half)], sem).start()


def arrive_down(target, sem):
    pltpu.make_async_copy(target, target, sem).wait()


def norm_scale(z):
    return lax.rsqrt(jnp.mean(z * z, axis=-1, keepdims=True) + epsilon)


def gain_row(tile):
    lane = lax.broadcasted_iota(jnp.int32, (8, LANES), 1)
    pick = jnp.where(lane == 0, 1.0, 0.0).astype(BF)
    return nt(pick, tile)[0:1]


def gain_tile(rows):
    return tn(rows.astype(BF), jnp.ones((rows.shape[0], LANES), BF)).astype(BF)


def wide(table, width):
    return jnp.concatenate([table] * (width // LANES), axis=1)


def low_half(width, rows):
    lane = lax.broadcasted_iota(jnp.int32, (rows, width), 1)
    return lax.rem(lane, HD) < HD // 2


def rot(a, cosine, sine):
    width = a.shape[1]
    up = pltpu.roll(a, HD // 2, 1)
    down = pltpu.roll(a, width - HD // 2, 1)
    turned = jnp.where(low_half(width, a.shape[0]), -down, up)
    return a * wide(cosine, width) + turned * wide(sine, width)


def rot_back(b, cosine, sine):
    width = b.shape[1]
    c = b * wide(sine, width)
    up = pltpu.roll(c, HD // 2, 1)
    down = pltpu.roll(c, width - HD // 2, 1)
    turned = jnp.where(low_half(width, b.shape[0]), down, -up)
    return b * wide(cosine, width) + turned


def attn_in_kernel(layer, idx, x, a_own, a_got, v_own, v_got, cos, sin, normed_out, q_out, kv_out, a_w, v_w, sems):
    own = idx[0] == layer
    fetch(own, a_own, a_got, a_w, sems.at[0])
    fetch(own, v_own, v_got, v_w, sems.at[1])
    z = x[...].astype(F32)
    scaled = z * norm_scale(z)
    arrive(a_own, a_w, sems.at[0])
    width = (HQ + HK) * HD
    gain = gain_row(a_w[:, width:])
    normed = (scaled * gain).astype(BF)
    normed_out[...] = normed
    qk = rot(nn(normed, a_w[:, :width]), cos[...], sin[...])
    q_out[...] = (qk[:, : HQ * HD].astype(BF).astype(F32) * HD ** (-0.5)).astype(BF)
    arrive(v_own, v_w, sems.at[1])
    value = nn(normed, v_w[:, :width])[:, HQ * HD :]
    kv_out[...] = jnp.concatenate([qk[:, HQ * HD :].astype(BF), value.astype(BF)], axis=1)


def attn_in(layer, idx, x, weights, cos, sin, after=()):
    rows, depth = x.shape
    a_own, a_got, v_own, v_got = weights
    args = (idx, x, a_own, a_got, v_own, v_got, cos, sin)
    return call(
        functools.partial(attn_in_kernel, layer),
        (shape((rows, depth), BF), shape((rows, HQ * HD), BF), shape((rows, 2 * HK * HD), BF)),
        [IN_SMEM, IN_VMEM] + [ANYWHERE] * 4 + [IN_VMEM] * 2,
        [pltpu.VMEM(a_own.shape, BF), pltpu.VMEM(v_own.shape, BF), pltpu.SemaphoreType.DMA((2,))],
        args,
        2 * rows * depth * 1536,
        after,
        limit=40,
    )


def score_block(keys, query, block, reach, causal):
    s = nt(keys, query)
    if block == 0:
        return jnp.where(causal, s, masked_score)
    return jnp.where(block <= reach, s, masked_score)


def causal_mask(rows):
    key_at = lax.broadcasted_iota(jnp.int32, (rows, rows), 0)
    query_at = lax.broadcasted_iota(jnp.int32, (rows, rows), 1)
    return key_at <= query_at


def head(values, at):
    return values[:, at * HD : (at + 1) * HD]


def attend_kernel(blocks, idx, q, *refs):
    kv = [r[...] for r in refs[:blocks]]
    attn_out, lse_out = refs[blocks:]
    rows = q.shape[0]
    reach = idx[1]
    causal = causal_mask(rows)
    queries = q[...]
    pieces = []
    lse_out[...] = jnp.zeros_like(lse_out)
    for g in range(HK):
        keys = [head(b, g) for b in kv]
        values = jnp.concatenate([head(b, HK + g) for b in kv], axis=0)
        for i in range(GROUP):
            h = g * GROUP + i
            query = head(queries, h)
            s = jnp.concatenate(
                [score_block(k, query, d, reach, causal) for d, k in enumerate(keys)], axis=0
            )
            top = jnp.max(s, axis=0, keepdims=True)
            p = jnp.exp(s - top)
            total = jnp.sum(p, axis=0, keepdims=True)
            lse_out[h : h + 1, :] = top + jnp.log(total)
            p_low = (p * (1.0 / total)).astype(BF)
            pieces.append(tn(p_low, values).astype(BF))
    attn_out[...] = jnp.concatenate(pieces, axis=1)


def attend(idx, q, kv, after=()):
    rows = q.shape[0]
    return call(
        functools.partial(attend_kernel, len(kv)),
        (shape((rows, HQ * HD), BF), shape((16, rows), F32)),
        [IN_SMEM] + [IN_VMEM] * (1 + len(kv)),
        [],
        (idx, q) + tuple(kv),
        2 * 2 * rows * rows * len(kv) * HQ * HD * 4,
        after,
        limit=40,
    )


def mlp_kernel(layer, parts, idx, x, attn, v_own, v_got, g_m, g_t, d_m, d_t, y_out, resid_out, mn_out, gate_out, up_out, hid_out, v_w, d_w, sems):
    own = idx[0] == layer
    first = idx[0] == 0
    fetch(own, v_own, v_got, v_w, sems.at[0])
    fetch_down(parts, idx[0], d_m, d_t, d_w, sems.at[1])
    arrive(v_own, v_w, sems.at[0])
    width = HQ * HD
    depth = x.shape[1]
    resid = x[...].astype(F32) + nn(attn[...], v_w[:, :depth])
    resid_out[...] = resid
    gain = gain_row(v_w[:, width + HK * HD :])
    mn = (resid * norm_scale(resid) * gain).astype(BF)
    mn_out[...] = mn
    mine = nn(mn, g_m[...])
    theirs = nn(mn, g_t[...])
    gate = jnp.where(first, mine, theirs)
    up = jnp.where(first, theirs, mine)
    gate_out[...] = gate
    up_out[...] = up
    hid = (gate * jax.nn.sigmoid(gate) * up).astype(BF)
    hid_out[...] = hid
    arrive_down(d_w, sems.at[1])
    y_out[...] = (resid + nn(hid, d_w[:, :depth])).astype(BF)


def mlp(layer, parts, idx, x, attn, weights, g_m, g_t, d_m, d_t, after=()):
    rows, depth = x.shape
    _, _, v_own, v_got = weights
    ff = g_m.shape[1]
    args = (idx, x, attn, v_own, v_got, g_m, g_t, d_m, d_t)
    return call(
        functools.partial(mlp_kernel, layer, parts),
        (
            shape((rows, depth), BF),
            shape((rows, depth), F32),
            shape((rows, depth), BF),
            shape((rows, ff), F32),
            shape((rows, ff), F32),
            shape((rows, ff), BF),
        ),
        [IN_SMEM, IN_VMEM, IN_VMEM] + [ANYWHERE] * 2 + [IN_VMEM] * 2 + [ANYWHERE] * 2,
        [
            pltpu.VMEM(v_own.shape, BF),
            pltpu.VMEM((ff, d_m.shape[1]), BF),
            pltpu.SemaphoreType.DMA((2,)),
        ],
        args,
        2 * rows * depth * (3 * ff + depth),
        after,
        limit=40,
    )


def mlp_back_kernel(layer, parts, idx, e, resid, gate, up, g_m, g_t, d_m, d_t, v_own, v_got, gm_out, gt_out, rg_out, mix_out, ag_out, mg_out, v_w, d_w, sems):
    own = idx[0] == layer
    first = idx[0] == 0
    fetch_down(parts, idx[0], d_m, d_t, d_w, sems.at[1])
    fetch(own, v_own, v_got, v_w, sems.at[0])
    low = e[...]
    arrive_down(d_w, sems.at[1])
    hg = nt(low, d_w[:, : e.shape[1]])
    gv = gate[...]
    sig = jax.nn.sigmoid(gv)
    g_in = (hg * up[...] * sig * (1.0 + gv * (1.0 - sig))).astype(BF)
    u_in = (hg * gv * sig).astype(BF)
    mine = jnp.where(first, g_in, u_in)
    theirs = jnp.where(first, u_in, g_in)
    gm_out[...] = mine
    gt_out[...] = theirs
    ng = nt(mine, g_m[...]) + nt(theirs, g_t[...])
    arrive(v_own, v_w, sems.at[0])
    width = HQ * HD
    depth = e.shape[1]
    gain = gain_row(v_w[:, width + HK * HD :])
    z = resid[...]
    inv = norm_scale(z)
    weighted = ng * gain
    mg_out[...] = gain_tile(ng * z * inv)
    part = inv * weighted - z * (inv * inv * inv) * jnp.mean(z * weighted, axis=-1, keepdims=True)
    rg = low.astype(F32) + part
    rg_out[...] = rg
    mix = rg.astype(BF)
    mix_out[...] = mix
    ag_out[...] = nt(mix, v_w[:, :depth]).astype(BF)


def mlp_back(layer, parts, idx, e, resid, gate, up, g_m, g_t, d_m, d_t, weights, after=()):
    rows, depth = e.shape
    _, _, v_own, v_got = weights
    ff = g_m.shape[1]
    args = (idx, e, resid, gate, up, g_m, g_t, d_m, d_t, v_own, v_got)
    return call(
        functools.partial(mlp_back_kernel, layer, parts),
        (
            shape((rows, ff), BF),
            shape((rows, ff), BF),
            shape((rows, depth), F32),
            shape((rows, depth), BF),
            shape((rows, HQ * HD), BF),
            shape((depth, LANES), BF),
        ),
        [IN_SMEM] + [IN_VMEM] * 6 + [ANYWHERE] * 4,
        [
            pltpu.VMEM(v_own.shape, BF),
            pltpu.VMEM((ff, d_m.shape[1]), BF),
            pltpu.SemaphoreType.DMA((2,)),
        ],
        args,
        2 * rows * depth * (3 * ff + depth),
        after,
        limit=40,
    )


def padded_rows(count, step=16):
    return count + -count % step


class Packing:
    def __init__(self, shard, half, ff, depth):
        self.shard = shard
        self.half = half
        self.shard_step = padded_rows(shard)
        self.half_step = padded_rows(half)
        self.gate_tiles = ff // LANES
        self.down_tiles = padded_rows(depth, LANES) // LANES
        self.out_tiles = (self.down_tiles + 1) // 2
        self.down_at = self.gate_tiles * self.shard_step
        self.out_at = self.down_at + self.down_tiles * self.half_step
        used = self.out_at + self.out_tiles * self.shard_step
        self.used = used
        self.rows = self.down_at + padded_rows(used - self.down_at, 64)
        self.entry_tiles = (HQ + 2 * HK + 1) * HD // LANES // 2
        self.entry_rows = self.entry_tiles * self.shard_step


def tile(value, at):
    return value[:, at * LANES : (at + 1) * LANES]


def mlp_grads_kernel(pack, idx, hid, e, mn, gm, gt, attn, mix, mg, m_out, t_out):
    parts = m_out.shape[0]
    first = idx[0] == 0
    depth = mn.shape[1]
    shard, half = pack.shard, pack.half
    mnv = mn[...]
    fill = pack.down_tiles * LANES - depth
    down = tn(hid[...], e[...]).astype(BF)
    down = jnp.concatenate([down, jnp.zeros((down.shape[0], fill), BF)], axis=1)
    outward = tn(attn[...], mix[...]).astype(BF)
    outward = jnp.concatenate([outward, mg[:, :fill]], axis=1)
    blank = jnp.zeros((shard, LANES), BF)
    for out, side, low in ((m_out, gm, first), (t_out, gt, jnp.logical_not(first))):
        gate = tn(mnv, side[...]).astype(BF)
        for f in range(parts):
            rows = slice(f * shard, (f + 1) * shard)
            for k in range(pack.gate_tiles):
                at = k * pack.shard_step
                out[f, at : at + shard, :] = tile(gate[rows], k)
            low_half = down[2 * f * half : (2 * f + 1) * half]
            high_half = down[(2 * f + 1) * half : (2 * f + 2) * half]
            own_half = jnp.where(low, low_half, high_half)
            for k in range(pack.down_tiles):
                at = pack.down_at + k * pack.half_step
                out[f, at : at + half, :] = tile(own_half, k)
            for k in range(pack.out_tiles):
                at = pack.out_at + k * pack.shard_step
                other = k + pack.out_tiles
                high = tile(outward[rows], other) if other < pack.down_tiles else blank
                out[f, at : at + shard, :] = jnp.where(low, tile(outward[rows], k), high)
            if pack.used < pack.rows:
                out[f, pack.used :, :] = jnp.zeros((pack.rows - pack.used, LANES), BF)


def mlp_grads(pack, parts, idx, hid, e, mn, gm, gt, attn, mix, mg, after=()):
    rows, depth = e.shape
    ff = gm.shape[1]
    return call(
        functools.partial(mlp_grads_kernel, pack),
        (shape((parts, pack.rows, LANES), BF), shape((parts, pack.rows, LANES), BF)),
        [IN_SMEM] + [IN_VMEM] * 8,
        [],
        (idx, hid, e, mn, gm, gt, attn, mix, mg),
        2 * rows * depth * (3 * ff + depth),
        after,
        limit=40,
    )


def halves(idx, zero, one, got):
    first = idx[0] == 0
    keep = jnp.where(first, zero[...], one[...])
    other = got[...]
    return jnp.where(first, keep, other), jnp.where(first, other, keep)


def gain_of(last_tile, shard):
    return last_tile.astype(F32).T[LANES - HD : LANES - HD + 1, :shard]


def unpack_mlp_kernel(pack, idx, zero, one, got, gate_out, up_out, down_out, o_out, gain_out):
    shard, half = pack.shard, pack.half
    both = halves(idx, zero, one, got)
    for value, out in zip(both, (gate_out, up_out)):
        for k in range(pack.gate_tiles):
            at = k * pack.shard_step
            out[:, k * LANES : (k + 1) * LANES] = value[at : at + shard].astype(F32)
    depth = down_out.shape[0]
    downs = []
    for side, value in enumerate(both):
        tiles = []
        for k in range(pack.down_tiles):
            at = pack.down_at + k * pack.half_step
            tiles.append(value[at : at + half])
        downs.append(jnp.concatenate(tiles, axis=1).astype(F32))
    down_out[...] = jnp.concatenate(downs, axis=0).T[:depth]
    tiles = []
    for k in range(pack.down_tiles):
        at = pack.out_at + (k % pack.out_tiles) * pack.shard_step
        tiles.append(both[k // pack.out_tiles][at : at + shard])
    o_out[...] = jnp.concatenate(tiles, axis=1)[:, :depth].astype(F32)
    at = pack.out_at + (pack.down_tiles - 1 - pack.out_tiles) * pack.shard_step
    gain_out[...] = gain_of(both[1][at : at + pack.shard_step], shard)


def unpack_mlp(pack, idx, zero, one, got, ff, depth):
    return call(
        functools.partial(unpack_mlp_kernel, pack),
        (
            shape((pack.shard, ff), F32),
            shape((pack.shard, ff), F32),
            shape((depth, 2 * pack.half), F32),
            shape((pack.shard, depth), F32),
            shape((1, pack.shard), F32),
        ),
        [IN_SMEM] + [IN_VMEM] * 3,
        [],
        (idx, zero, one, got),
        1000,
    )


def unpack_entry_kernel(pack, idx, zero, one, got, q_out, k_out, v_out, gain_out):
    shard = pack.shard
    tiles = []
    both = halves(idx, zero, one, got)
    for value in both:
        for k in range(pack.entry_tiles):
            at = k * pack.shard_step
            tiles.append(value[at : at + shard])
    full = jnp.concatenate(tiles, axis=1).astype(F32)
    qw, kw = HQ * HD, HK * HD
    q_out[...] = full[:, :qw]
    k_out[...] = full[:, qw : qw + kw]
    v_out[...] = full[:, qw + kw : qw + 2 * kw]
    at = (pack.entry_tiles - 1) * pack.shard_step
    gain_out[...] = gain_of(both[1][at : at + pack.shard_step], shard)


def unpack_entry(pack, idx, zero, one, got):
    qw, kw = HQ * HD, HK * HD
    return call(
        functools.partial(unpack_entry_kernel, pack),
        (
            shape((pack.shard, qw), F32),
            shape((pack.shard, kw), F32),
            shape((pack.shard, kw), F32),
            shape((1, pack.shard), F32),
        ),
        [IN_SMEM] + [IN_VMEM] * 3,
        [],
        (idx, zero, one, got),
        1000,
    )


def attend_back_kernel(blocks, idx, q, ag, lse, *refs):
    kv = [r[...] for r in refs[:blocks]]
    dq_out, own_out = refs[blocks : blocks + 2]
    far_out = refs[blocks + 2 :]
    rows = q.shape[0]
    reach = idx[1]
    causal = causal_mask(rows)
    queries = q[...]
    grads = ag[...]
    dq_parts = []
    dk_parts = []
    dv_parts = []
    for g in range(HK):
        keys = [head(b, g) for b in kv]
        all_keys = jnp.concatenate(keys, axis=0)
        values = jnp.concatenate([head(b, HK + g) for b in kv], axis=0)
        dk = None
        dv = None
        for i in range(GROUP):
            h = g * GROUP + i
            query = head(queries, h)
            grad = head(grads, h)
            s = jnp.concatenate(
                [score_block(k, query, d, reach, causal) for d, k in enumerate(keys)], axis=0
            )
            p = jnp.exp(s - lse[h : h + 1, :])
            dp = nt(values, grad)
            delta = jnp.sum(p * dp, axis=0, keepdims=True)
            ds = (p * (dp - delta)).astype(BF)
            dv_h = nn(p.astype(BF), grad)
            dk_h = nn(ds, query)
            dk = dk_h if dk is None else dk + dk_h
            dv = dv_h if dv is None else dv + dv_h
            dq_parts.append(tn(ds, all_keys) * HD ** (-0.5))
        dk_parts.append(dk)
        dv_parts.append(dv)
    dq_out[...] = jnp.concatenate(dq_parts, axis=1)
    joined = jnp.concatenate(dk_parts + dv_parts, axis=1)
    own_out[...] = joined[:rows]
    for d, out in enumerate(far_out):
        out[...] = joined[(d + 1) * rows : (d + 2) * rows].astype(BF)


def attend_back(idx, q, ag, lse, kv, after=()):
    rows = q.shape[0]
    outs = [shape((rows, HQ * HD), F32), shape((rows, 2 * HK * HD), F32)]
    outs += [shape((rows, 2 * HK * HD), BF) for _ in kv[1:]]
    return call(
        functools.partial(attend_back_kernel, len(kv)),
        outs,
        [IN_SMEM] + [IN_VMEM] * (3 + len(kv)),
        [],
        (idx, q, ag, lse) + tuple(kv),
        5 * 2 * rows * rows * len(kv) * HQ * HD * 4,
        after,
    )


def input_back_kernel(layer, pack, far, idx, x, normed, dq, own_kv, *refs):
    far_kv = refs[:far]
    rg, a_own, a_got, v_own, v_got, cos, sin, ig_out, m_out, t_out, a_w, v_w, sems = refs[far:]
    own = idx[0] == layer
    first = idx[0] == 0
    fetch(own, a_own, a_got, a_w, sems.at[0])
    fetch(own, v_own, v_got, v_w, sems.at[1])
    kv = own_kv[...]
    for r in far_kv:
        kv = kv + r[...].astype(F32)
    half = HK * HD
    qk = jnp.concatenate([dq[...], kv[:, :half]], axis=1)
    qk_in = rot_back(qk, cos[...], sin[...]).astype(BF)
    v_in = kv[:, half:].astype(BF)
    rows, depth = x.shape
    width = (HQ + HK) * HD
    padded = jnp.concatenate([jnp.zeros((rows, HQ * HD), BF), v_in], axis=1)
    arrive(a_own, a_w, sems.at[0])
    arrive(v_own, v_w, sems.at[1])
    ng = nt(qk_in, a_w[:, :width]) + nt(padded, v_w[:, :width])
    z = x[...].astype(F32)
    gain = gain_row(a_w[:, width:])
    inv = norm_scale(z)
    weighted = ng * gain
    part = inv * weighted - z * (inv * inv * inv) * jnp.mean(z * weighted, axis=-1, keepdims=True)
    ig_out[...] = (rg[...] + part).astype(BF)
    nv = normed[...]
    grads = jnp.concatenate(
        [
            tn(nv, qk_in).astype(BF),
            tn(nv, v_in).astype(BF),
            gain_tile(ng * z * inv)[:, :HD],
        ],
        axis=1,
    )
    shard = pack.shard
    for f in range(m_out.shape[0]):
        piece = grads[f * shard : (f + 1) * shard]
        for k in range(pack.entry_tiles):
            at = k * pack.shard_step
            low = tile(piece, k)
            high = tile(piece, k + pack.entry_tiles)
            m_out[f, at : at + shard, :] = jnp.where(first, low, high)
            t_out[f, at : at + shard, :] = jnp.where(first, high, low)


def input_back(layer, pack, parts, idx, x, normed, dq, own_kv, far_kv, rg, weights, cos, sin, after=()):
    rows, depth = x.shape
    a_own, a_got, v_own, v_got = weights
    args = (idx, x, normed, dq, own_kv) + tuple(far_kv)
    args += (rg, a_own, a_got, v_own, v_got, cos, sin)
    packed = (parts, pack.entry_rows, LANES)
    return call(
        functools.partial(input_back_kernel, layer, pack, len(far_kv)),
        (shape((rows, depth), BF), shape(packed, BF), shape(packed, BF)),
        [IN_SMEM] + [IN_VMEM] * (5 + len(far_kv)) + [ANYWHERE] * 4 + [IN_VMEM] * 2,
        [pltpu.VMEM(a_own.shape, BF), pltpu.VMEM(v_own.shape, BF), pltpu.SemaphoreType.DMA((2,))],
        args,
        2 * 2 * rows * depth * 1536,
        after,
    )


def crossed(value, axis, mask):
    count = lax.axis_size(axis)
    return lax.ppermute(value, axis, [(i, i ^ mask) for i in range(count)])


def shifted(value, distance):
    devices = range(lax.axis_size("ctx"))
    return lax.ppermute(value, "ctx", [(i, i + distance) for i in devices if i + distance in devices])


def other_core(value):
    return crossed(value, "section", 1)


def bits_of(count):
    return [b for b in range(count.bit_length() - 1)]


def held(value, *deps):
    return lax.optimization_barrier((value,) + deps)[0]


def gather_step(value, have, bit, wait):
    me = lax.axis_index("fsdp")
    got = crossed(value, "fsdp", 1 << bit)
    if wait:
        got = held(got, *wait)
    low = ((me >> bit) & 1) == 0
    place = sum(1 for b in have if b > bit)
    return jnp.stack([jnp.where(low, value, got), jnp.where(low, got, value)], axis=place)


def gather_some(values, orders, first, last, wait=()):
    for step in range(first, last):
        late = wait if step == last - 1 else ()
        values = [gather_step(v, o[:step], o[step], late) for v, o in zip(values, orders)]
    return values


def whole_rows(value):
    return value.reshape((value.size // value.shape[-1],) + value.shape[-1:])


def cut(value, left, bit):
    mine = (lax.axis_index("fsdp") >> bit) & 1
    place = sorted(left, reverse=True).index(bit)
    send = lax.dynamic_index_in_dim(value, 1 - mine, place, keepdims=False)
    keep = lax.dynamic_index_in_dim(value, mine, place, keepdims=False)
    return send, keep


def added(halves, bit, wait=()):
    send, keep = halves
    got = crossed(send, "fsdp", 1 << bit)
    if wait:
        got = held(got, *wait)
    return (keep.astype(F32) + got.astype(F32)).astype(BF)


def first_cut(value, order):
    count = lax.axis_size("fsdp")
    value = value.reshape((2,) * len(order) + (value.shape[0] // count,) + value.shape[1:])
    return cut(value, order, order[0])


def scatter_rest(value, order, wait=()):
    for step in range(1, len(order)):
        late = wait if step == len(order) - 1 else ()
        value = added(cut(value, order[step:], order[step]), order[step], late)
    return value


def sum_over_ctx(value):
    count = lax.axis_size("ctx")
    if count & (count - 1):
        return lax.psum(value, "ctx")
    for bit in bits_of(count):
        value = (value.astype(F32) + crossed(value, "ctx", 1 << bit).astype(F32)).astype(BF)
    return value


def ctx_cut(value):
    me = lax.axis_index("ctx") & 1
    size = value.shape[0] // 2
    send = lax.dynamic_slice_in_dim(value, (1 - me) * size, size, 0)
    keep = lax.dynamic_slice_in_dim(value, me * size, size, 0)
    return send, keep


def ctx_begin(halves, wait=()):
    send, keep = halves
    got = crossed(send, "ctx", 1)
    if wait:
        got = held(got, *wait)
    return (keep.astype(F32) + got.astype(F32)).astype(BF)


def ctx_middle(value, wait=()):
    for bit in bits_of(lax.axis_size("ctx"))[1:]:
        value = added_over_ctx(value, bit, wait)
    return value


def ctx_end(value, wait=()):
    low = (lax.axis_index("ctx") & 1) == 0
    got = crossed(value, "ctx", 1)
    if wait:
        got = held(got, *wait)
    return jnp.concatenate([jnp.where(low, value, got), jnp.where(low, got, value)], axis=0)


def added_over_ctx(value, bit, wait):
    got = crossed(value, "ctx", 1 << bit)
    if wait:
        got = held(got, *wait)
    return (value.astype(F32) + got.astype(F32)).astype(BF)


def body(
    inputs,
    positions,
    out_grad,
    attn_gain,
    query_proj,
    key_proj,
    value_proj,
    out_proj,
    mlp_gain,
    gate_proj,
    up_proj,
    down_proj,
):
    core = lax.axis_index("section")
    first = core == 0
    ctx = lax.axis_index("ctx")
    ctx_count = lax.axis_size("ctx")
    fsdp_count = lax.axis_size("fsdp")
    micro, seqs, block, depth = inputs.shape
    shard = query_proj.shape[1]
    rows = seqs * block
    idx = jnp.stack([core, ctx]).astype(jnp.int32)
    up_order = bits_of(fsdp_count)
    down_order = up_order[::-1]

    def pick(a, b):
        return jnp.where(first, a, b)

    def tile_of(gain):
        return jnp.broadcast_to(gain[0][:, None], (shard, LANES))

    a_piece = jnp.concatenate([query_proj[0], key_proj[0], tile_of(attn_gain)], axis=1)
    v_piece = jnp.concatenate([out_proj[0], value_proj[0], tile_of(mlp_gain)], axis=1)
    steps = len(up_order)
    a_own, v_own = gather_some([a_piece, v_piece], [up_order, down_order], 0, steps)
    a_own = whole_rows(a_own)
    v_own = whole_rows(v_own)
    a_got = other_core(a_own)
    v_got = other_core(v_own)
    attn_w = (a_own, a_got, v_own, v_got)

    half = down_proj.shape[1] // 2
    g_keep = pick(gate_proj[0], up_proj[0])
    g_got = other_core(pick(up_proj[0], gate_proj[0]))
    wide_down = jnp.pad(down_proj[0], ((0, 0), (0, -depth % LANES)))
    d_keep = pick(wide_down[:half], wide_down[half:])
    d_got = other_core(pick(wide_down[half:], wide_down[:half]))
    def feed_forward_pieces(layer):
        g_piece = pick(g_keep, g_got) if layer == 0 else pick(g_got, g_keep)
        d_piece = pick(d_keep, d_got) if layer == 0 else pick(d_got, d_keep)
        return [g_piece, d_piece]

    parts_of_down = fsdp_count if half % 16 == 0 else 0

    def down_halves(mine, theirs):
        if parts_of_down:
            return (mine, theirs)
        mine, theirs = [v.reshape(fsdp_count, half, -1) for v in (mine, theirs)]
        full = jnp.stack([pick(mine, theirs), pick(theirs, mine)], axis=1)
        full = whole_rows(full)
        return (full, full)

    places = lax.dynamic_index_in_dim(positions, core, 0, keepdims=False).reshape(rows)
    frequency = rope_base ** (-(jnp.arange(HD // 2, dtype=F32) * 2.0 / HD))
    angles = places.astype(F32)[:, None] * frequency
    cos = jnp.concatenate([jnp.cos(angles)] * 4, axis=-1)
    sin = jnp.concatenate([jnp.sin(angles)] * 4, axis=-1)

    x = lax.dynamic_index_in_dim(inputs, core, 0, keepdims=False).reshape(rows, depth)
    saved = []
    ff_w = [None, None]
    for layer in range(2):
        normed, q, kv_own = attn_in(layer, idx, x, attn_w, cos, sin)
        kv = [kv_own] + [shifted(kv_own, d) for d in range(1, ctx_count)]
        orders = [up_order, down_order] if layer == 0 else [down_order, up_order]
        if layer == 0:
            parts = lax.optimization_barrier(tuple(feed_forward_pieces(0)) + (a_own, v_own))[:2]
        parts = gather_some(parts, orders, 0, 1, (normed,))
        if layer == 1:
            parts = lax.optimization_barrier(tuple(parts) + (normed,))[:2]
        g_all, d_all = gather_some(parts, orders, 1, steps)
        attn, lse = attend(idx, q, kv)
        g_all, d_all, attn = lax.optimization_barrier((whole_rows(g_all), whole_rows(d_all), attn))
        ff_w[layer] = (g_all, other_core(g_all)) + down_halves(d_all, other_core(d_all))
        if layer == 0:
            parts = lax.optimization_barrier(tuple(feed_forward_pieces(1)) + (g_all, d_all))[:2]
        y, resid, mn, gate, up, hid = mlp(layer, parts_of_down, idx, x, attn, attn_w, *ff_w[layer])
        saved.append((x, normed, q, kv, attn, lse, resid, mn, gate, up, hid))
        x = y
    outs = [saved[1][0], x]

    pack = Packing(shard, half, gate_proj.shape[2], depth)

    def joined(mine, theirs, wait=()):
        got = other_core(theirs)
        if wait:
            got = held(got, *wait)
        return (mine.astype(F32) + got.astype(F32)).astype(BF)

    e = lax.dynamic_index_in_dim(out_grad, core, 0, keepdims=False).reshape(rows, depth)
    entry = [None, None]
    def feed_forward_back(layer, e, after, between):
        x, normed, q, kv, attn, lse, resid, mn, gate, up, hid = saved[layer]
        gm, gt, rg, mix, ag, mg = mlp_back(
            layer, parts_of_down, idx, e, resid, gate, up, *ff_w[layer], attn_w, after
        )
        done = tuple(between(ag)) if between else ()
        mine, theirs = mlp_grads(pack, fsdp_count, idx, hid, e, mn, gm, gt, attn, mix, mg, done)
        return rg, ag, mine, theirs

    def attention_back(layer, ag, after):
        x, normed, q, kv, attn, lse, resid, mn, gate, up, hid = saved[layer]
        back = attend_back(idx, q, ag, lse, kv, after)
        far_kv = [shifted(part, -(d + 1)) for d, part in enumerate(back[2:])]
        return back[0], back[1], far_kv

    def entry_back(layer, dq, own_kv, far_kv, rg, after):
        x, normed = saved[layer][:2]
        e, mine, theirs = input_back(
            layer, pack, fsdp_count, idx, x, normed, dq, own_kv, far_kv, rg, attn_w, cos, sin, after
        )
        entry[layer] = e
        return e, mine, theirs

    orders = (up_order, down_order)

    def start(value, at):
        return [first_cut(value[:, :at], up_order), first_cut(value[:, at:], down_order)]

    def sends(cuts):
        return tuple(c[0] for c in cuts)

    def first_sums(cuts, wait):
        return [added(c, o[0], wait) for c, o in zip(cuts, orders)]

    def last_sums(values, wait):
        values = [scatter_rest(v, o, wait) for v, o in zip(values, orders)]
        return jnp.concatenate(values, axis=1)[0]

    def next_cuts(values):
        return [cut(v, o[1:], o[1]) for v, o in zip(values, orders)] if steps > 1 else [values]

    middle = pack.down_at
    entry_middle = pack.entry_rows // 2
    rg, ag, mine, theirs = feed_forward_back(1, e, (), None)
    dq, own_kv, far_kv = attention_back(1, ag, (mine,))
    m1 = start(joined(mine, theirs, (dq,)), middle)
    e, a_mine, a_theirs = entry_back(1, dq, own_kv, far_kv, rg, sends(m1))
    m1 = first_sums(m1, (e,))

    def between(ag):
        m1_cut.extend(ctx_cut(last_sums(m1, (ag,))))
        return m1_cut[:1]

    m1_cut = []
    rg, ag, mine, theirs = feed_forward_back(0, e, tuple(m1), between)
    m0 = start(joined(mine, theirs), middle)
    m1 = ctx_begin(m1_cut, (m0[0][0],))
    dq, own_kv, far_kv = attention_back(0, ag, sends(m0) + (m1,))
    a1 = start(joined(a_mine, a_theirs, (dq,)), entry_middle)
    m0 = first_sums(m0, (dq,))
    m1 = ctx_middle(m1, (far_kv[-1],))
    e, a_mine, a_theirs = entry_back(
        0, dq, own_kv, far_kv, rg, sends(next_cuts(m0)) + sends(a1) + (m1,)
    )
    a0 = start(joined(a_mine, a_theirs), entry_middle)
    late = sends(a0)[0]
    m1 = held(m1, late)
    m0 = ctx_cut(last_sums(m0, (late,)))
    a1 = first_sums(a1, (m0[0],))
    a0 = first_sums(a0, (m0[0],))
    m0 = ctx_begin(m0, tuple(a0))
    a1 = last_sums(a1, (m0,))
    a0 = last_sums(a0, (m0,))
    m1 = ctx_end(m1, (a0,))
    a0 = ctx_begin(ctx_cut(jnp.concatenate([a0, a1], axis=0)), ())
    m0 = ctx_middle(m0, (a0,))
    a0 = ctx_middle(a0, (m0,))
    a0 = ctx_end(a0)
    a0, a1 = a0[: pack.entry_rows], a0[pack.entry_rows :]

    def own_layer(zero, one):
        keep = pick(zero, one)
        got = other_core(pick(one, zero))
        return (pick(keep, got), pick(got, keep))

    outs[0], outs[1], entry[0], entry[1], _ = lax.optimization_barrier(
        (outs[0], outs[1], entry[0], entry[1], late)
    )
    section_out = jnp.stack(own_layer(outs[0], outs[1])).reshape(1, micro, seqs, block, depth)
    input_grad = jnp.stack(own_layer(entry[0], entry[1])).reshape(1, micro, seqs, block, depth)
    ff = gate_proj.shape[2]
    a_got = other_core(pick(a1, a0))
    query_g, key_g, value_g, attn_gain_g = unpack_entry(pack, idx, a0, a1, a_got)
    m0 = ctx_end(m0, (query_g, section_out, input_grad))
    m_got = other_core(pick(m1, m0))
    gate_g, up_g, down_g, out_g, mlp_gain_g = unpack_mlp(pack, idx, m0, m1, m_got, ff, depth)

    return (
        section_out,
        input_grad,
        attn_gain_g,
        query_g[None],
        key_g[None],
        value_g[None],
        out_g[None],
        mlp_gain_g,
        gate_g[None],
        up_g[None],
        down_g.T[None],
    )


def solution(mesh):
    rows = P(None, "fsdp", "ctx", None)
    both = P("section", None, "fsdp", "ctx", None)
    vec = P("section", "fsdp")
    mat = P("section", "fsdp", None)
    return jax.shard_map(
        body,
        mesh=mesh,
        in_specs=(rows, P(None, "fsdp", "ctx"), rows, vec, mat, mat, mat, mat, vec, mat, mat, mat),
        out_specs=(both, both, vec, mat, mat, mat, mat, vec, mat, mat, mat),
        check_vma=False,
    )
```

```python
import functools

import jax
import jax.numpy as jnp
from jax import lax
from jax.experimental import pallas as pl
from jax.experimental.pallas import tpu as pltpu
from jax.sharding import PartitionSpec as P

HQ = 9
HK = 3
HD = 64
GROUP = HQ // HK
LANES = 128

epsilon = 1e-05
rope_base = 100000.0
masked_score = -1e30

BF = jnp.bfloat16
F32 = jnp.float32
MIB = 1024 * 1024

IN_VMEM = pl.BlockSpec(memory_space=pltpu.VMEM)
IN_SMEM = pl.BlockSpec(memory_space=pltpu.SMEM)
ANYWHERE = pl.BlockSpec(memory_space=pl.ANY)


def nn(a, b):
    return lax.dot_general(a, b, (((1,), (0,)), ((), ())), preferred_element_type=F32)


def nt(a, b):
    return lax.dot_general(a, b, (((1,), (1,)), ((), ())), preferred_element_type=F32)


def tn(a, b):
    return lax.dot_general(a, b, (((0,), (0,)), ((), ())), preferred_element_type=F32)


def shape(dims, kind):
    return jax.ShapeDtypeStruct(dims, kind)


def call(kernel, outs, in_specs, scratch, args, flops, after=(), limit=56):
    count = len(args)
    late = len(after)
    inner = kernel

    def kernel(*refs):
        inner(*refs[:count], *refs[count + late :])

    in_specs = list(in_specs) + [ANYWHERE] * late
    moved = sum(a.size * a.dtype.itemsize for a in args)
    moved += sum(o.size * o.dtype.itemsize for o in outs)
    return pl.pallas_call(
        kernel,
        out_shape=tuple(outs),
        in_specs=in_specs,
        out_specs=tuple(IN_VMEM for _ in outs),
        scratch_shapes=scratch,
        compiler_params=pltpu.CompilerParams(vmem_limit_bytes=limit * MIB),
        cost_estimate=pl.CostEstimate(flops=flops // 1000, bytes_accessed=moved // 1000, transcendentals=0),
    )(*args, *after)


def fetch(flag, yes_ref, no_ref, target, sem):
    @pl.when(flag)
    def _():
        pltpu.make_async_copy(yes_ref, target, sem).start()

    @pl.when(jnp.logical_not(flag))
    def _():
        pltpu.make_async_copy(no_ref, target, sem).start()


def arrive(ref, target, sem):
    pltpu.make_async_copy(ref, target, sem).wait()


def fetch_down(parts, core, mine, theirs, target, sem):
    if parts == 0:
        pltpu.make_async_copy(mine, target, sem).start()
        return
    half = mine.shape[0] // parts
    for i in range(parts):
        rows = pl.ds(i * half, half)
        for source, place in ((mine, core), (theirs, 1 - core)):
            start = pl.multiple_of((2 * i + place) * half, half)
            pltpu.make_async_copy(source.at[rows], target.at[pl.ds(start, half)], sem).start()


def arrive_down(target, sem):
    pltpu.make_async_copy(target, target, sem).wait()


def norm_scale(z):
    return lax.rsqrt(jnp.mean(z * z, axis=-1, keepdims=True) + epsilon)


def gain_row(tile):
    lane = lax.broadcasted_iota(jnp.int32, (8, LANES), 1)
    pick = jnp.where(lane == 0, 1.0, 0.0).astype(BF)
    return nt(pick, tile)[0:1]


def gain_tile(rows):
    return tn(rows.astype(BF), jnp.ones((rows.shape[0], LANES), BF)).astype(BF)


def wide(table, width):
    return jnp.concatenate([table] * (width // LANES), axis=1)


def low_half(width, rows):
    lane = lax.broadcasted_iota(jnp.int32, (rows, width), 1)
    return lax.rem(lane, HD) < HD // 2


def rot(a, cosine, sine):
    width = a.shape[1]
    up = pltpu.roll(a, HD // 2, 1)
    down = pltpu.roll(a, width - HD // 2, 1)
    turned = jnp.where(low_half(width, a.shape[0]), -down, up)
    return a * wide(cosine, width) + turned * wide(sine, width)


def rot_back(b, cosine, sine):
    width = b.shape[1]
    c = b * wide(sine, width)
    up = pltpu.roll(c, HD // 2, 1)
    down = pltpu.roll(c, width - HD // 2, 1)
    turned = jnp.where(low_half(width, b.shape[0]), down, -up)
    return b * wide(cosine, width) + turned


def attn_in_kernel(layer, idx, x, a_own, a_got, v_own, v_got, cos, sin, normed_out, q_out, kv_out, a_w, v_w, sems):
    own = idx[0] == layer
    fetch(own, a_own, a_got, a_w, sems.at[0])
    fetch(own, v_own, v_got, v_w, sems.at[1])
    z = x[...].astype(F32)
    scaled = z * norm_scale(z)
    arrive(a_own, a_w, sems.at[0])
    width = (HQ + HK) * HD
    gain = gain_row(a_w[:, width:])
    normed = (scaled * gain).astype(BF)
    normed_out[...] = normed
    qk = rot(nn(normed, a_w[:, :width]), cos[...], sin[...])
    q_out[...] = (qk[:, : HQ * HD].astype(BF).astype(F32) * HD ** (-0.5)).astype(BF)
    arrive(v_own, v_w, sems.at[1])
    value = nn(normed, v_w[:, :width])[:, HQ * HD :]
    kv_out[...] = jnp.concatenate([qk[:, HQ * HD :].astype(BF), value.astype(BF)], axis=1)


def attn_in(layer, idx, x, weights, cos, sin, after=()):
    rows, depth = x.shape
    a_own, a_got, v_own, v_got = weights
    args = (idx, x, a_own, a_got, v_own, v_got, cos, sin)
    return call(
        functools.partial(attn_in_kernel, layer),
        (shape((rows, depth), BF), shape((rows, HQ * HD), BF), shape((rows, 2 * HK * HD), BF)),
        [IN_SMEM, IN_VMEM] + [ANYWHERE] * 4 + [IN_VMEM] * 2,
        [pltpu.VMEM(a_own.shape, BF), pltpu.VMEM(v_own.shape, BF), pltpu.SemaphoreType.DMA((2,))],
        args,
        2 * rows * depth * 1536,
        after,
        limit=40,
    )


def score_block(keys, query, block, reach, causal):
    s = nt(keys, query)
    if block == 0:
        return jnp.where(causal, s, masked_score)
    return jnp.where(block <= reach, s, masked_score)


def causal_mask(rows):
    key_at = lax.broadcasted_iota(jnp.int32, (rows, rows), 0)
    query_at = lax.broadcasted_iota(jnp.int32, (rows, rows), 1)
    return key_at <= query_at


def head(values, at):
    return values[:, at * HD : (at + 1) * HD]


def attend_kernel(blocks, idx, q, *refs):
    kv = [r[...] for r in refs[:blocks]]
    attn_out, lse_out = refs[blocks:]
    rows = q.shape[0]
    reach = idx[1]
    causal = causal_mask(rows)
    queries = q[...]
    pieces = []
    lse_out[...] = jnp.zeros_like(lse_out)
    for g in range(HK):
        keys = [head(b, g) for b in kv]
        values = jnp.concatenate([head(b, HK + g) for b in kv], axis=0)
        for i in range(GROUP):
            h = g * GROUP + i
            query = head(queries, h)
            s = jnp.concatenate(
                [score_block(k, query, d, reach, causal) for d, k in enumerate(keys)], axis=0
            )
            top = jnp.max(s, axis=0, keepdims=True)
            p = jnp.exp(s - top)
            total = jnp.sum(p, axis=0, keepdims=True)
            lse_out[h : h + 1, :] = top + jnp.log(total)
            p_low = (p * (1.0 / total)).astype(BF)
            pieces.append(tn(p_low, values).astype(BF))
    attn_out[...] = jnp.concatenate(pieces, axis=1)


def attend(idx, q, kv, after=()):
    rows = q.shape[0]
    return call(
        functools.partial(attend_kernel, len(kv)),
        (shape((rows, HQ * HD), BF), shape((16, rows), F32)),
        [IN_SMEM] + [IN_VMEM] * (1 + len(kv)),
        [],
        (idx, q) + tuple(kv),
        2 * 2 * rows * rows * len(kv) * HQ * HD * 4,
        after,
        limit=40,
    )


def mlp_kernel(layer, parts, idx, x, attn, v_own, v_got, g_m, g_t, d_m, d_t, y_out, resid_out, mn_out, gate_out, up_out, hid_out, v_w, d_w, sems):
    own = idx[0] == layer
    first = idx[0] == 0
    fetch(own, v_own, v_got, v_w, sems.at[0])
    fetch_down(parts, idx[0], d_m, d_t, d_w, sems.at[1])
    arrive(v_own, v_w, sems.at[0])
    width = HQ * HD
    depth = x.shape[1]
    resid = x[...].astype(F32) + nn(attn[...], v_w[:, :depth])
    resid_out[...] = resid
    gain = gain_row(v_w[:, width + HK * HD :])
    mn = (resid * norm_scale(resid) * gain).astype(BF)
    mn_out[...] = mn
    mine = nn(mn, g_m[...])
    theirs = nn(mn, g_t[...])
    gate = jnp.where(first, mine, theirs)
    up = jnp.where(first, theirs, mine)
    gate_out[...] = gate
    up_out[...] = up
    hid = (gate * jax.nn.sigmoid(gate) * up).astype(BF)
    hid_out[...] = hid
    arrive_down(d_w, sems.at[1])
    y_out[...] = (resid + nn(hid, d_w[:, :depth])).astype(BF)


def mlp(layer, parts, idx, x, attn, weights, g_m, g_t, d_m, d_t, after=()):
    rows, depth = x.shape
    _, _, v_own, v_got = weights
    ff = g_m.shape[1]
    args = (idx, x, attn, v_own, v_got, g_m, g_t, d_m, d_t)
    return call(
        functools.partial(mlp_kernel, layer, parts),
        (
            shape((rows, depth), BF),
            shape((rows, depth), F32),
            shape((rows, depth), BF),
            shape((rows, ff), F32),
            shape((rows, ff), F32),
            shape((rows, ff), BF),
        ),
        [IN_SMEM, IN_VMEM, IN_VMEM] + [ANYWHERE] * 2 + [IN_VMEM] * 2 + [ANYWHERE] * 2,
        [
            pltpu.VMEM(v_own.shape, BF),
            pltpu.VMEM((ff, d_m.shape[1]), BF),
            pltpu.SemaphoreType.DMA((2,)),
        ],
        args,
        2 * rows * depth * (3 * ff + depth),
        after,
        limit=40,
    )


def mlp_back_kernel(layer, parts, idx, e, resid, gate, up, g_m, g_t, d_m, d_t, v_own, v_got, gm_out, gt_out, rg_out, mix_out, ag_out, mg_out, v_w, d_w, sems):
    own = idx[0] == layer
    first = idx[0] == 0
    fetch_down(parts, idx[0], d_m, d_t, d_w, sems.at[1])
    fetch(own, v_own, v_got, v_w, sems.at[0])
    low = e[...]
    arrive_down(d_w, sems.at[1])
    hg = nt(low, d_w[:, : e.shape[1]])
    gv = gate[...]
    sig = jax.nn.sigmoid(gv)
    g_in = (hg * up[...] * sig * (1.0 + gv * (1.0 - sig))).astype(BF)
    u_in = (hg * gv * sig).astype(BF)
    mine = jnp.where(first, g_in, u_in)
    theirs = jnp.where(first, u_in, g_in)
    gm_out[...] = mine
    gt_out[...] = theirs
    ng = nt(mine, g_m[...]) + nt(theirs, g_t[...])
    arrive(v_own, v_w, sems.at[0])
    width = HQ * HD
    depth = e.shape[1]
    gain = gain_row(v_w[:, width + HK * HD :])
    z = resid[...]
    inv = norm_scale(z)
    weighted = ng * gain
    mg_out[...] = gain_tile(ng * z * inv)
    part = inv * weighted - z * (inv * inv * inv) * jnp.mean(z * weighted, axis=-1, keepdims=True)
    rg = low.astype(F32) + part
    rg_out[...] = rg
    mix = rg.astype(BF)
    mix_out[...] = mix
    ag_out[...] = nt(mix, v_w[:, :depth]).astype(BF)


def mlp_back(layer, parts, idx, e, resid, gate, up, g_m, g_t, d_m, d_t, weights, after=()):
    rows, depth = e.shape
    _, _, v_own, v_got = weights
    ff = g_m.shape[1]
    args = (idx, e, resid, gate, up, g_m, g_t, d_m, d_t, v_own, v_got)
    return call(
        functools.partial(mlp_back_kernel, layer, parts),
        (
            shape((rows, ff), BF),
            shape((rows, ff), BF),
            shape((rows, depth), F32),
            shape((rows, depth), BF),
            shape((rows, HQ * HD), BF),
            shape((depth, LANES), BF),
        ),
        [IN_SMEM] + [IN_VMEM] * 6 + [ANYWHERE] * 4,
        [
            pltpu.VMEM(v_own.shape, BF),
            pltpu.VMEM((ff, d_m.shape[1]), BF),
            pltpu.SemaphoreType.DMA((2,)),
        ],
        args,
        2 * rows * depth * (3 * ff + depth),
        after,
        limit=40,
    )


def padded_rows(count, step=16):
    return count + -count % step


class Packing:
    def __init__(self, shard, half, ff, depth):
        self.shard = shard
        self.half = half
        self.shard_step = padded_rows(shard)
        self.half_step = padded_rows(half)
        self.gate_tiles = ff // LANES
        self.down_tiles = padded_rows(depth, LANES) // LANES
        self.out_tiles = (self.down_tiles + 1) // 2
        self.down_at = self.gate_tiles * self.shard_step
        self.out_at = self.down_at + self.down_tiles * self.half_step
        used = self.out_at + self.out_tiles * self.shard_step
        self.used = used
        self.rows = self.down_at + padded_rows(used - self.down_at, 64)
        self.entry_tiles = (HQ + 2 * HK + 1) * HD // LANES // 2
        self.entry_rows = self.entry_tiles * self.shard_step


def tile(value, at):
    return value[:, at * LANES : (at + 1) * LANES]


def mlp_grads_kernel(pack, idx, hid, e, mn, gm, gt, attn, mix, mg, m_out, t_out):
    parts = m_out.shape[0]
    first = idx[0] == 0
    depth = mn.shape[1]
    shard, half = pack.shard, pack.half
    mnv = mn[...]
    fill = pack.down_tiles * LANES - depth
    down = tn(hid[...], e[...]).astype(BF)
    down = jnp.concatenate([down, jnp.zeros((down.shape[0], fill), BF)], axis=1)
    outward = tn(attn[...], mix[...]).astype(BF)
    outward = jnp.concatenate([outward, mg[:, :fill]], axis=1)
    blank = jnp.zeros((shard, LANES), BF)
    for out, side, low in ((m_out, gm, first), (t_out, gt, jnp.logical_not(first))):
        gate = tn(mnv, side[...]).astype(BF)
        for f in range(parts):
            rows = slice(f * shard, (f + 1) * shard)
            for k in range(pack.gate_tiles):
                at = k * pack.shard_step
                out[f, at : at + shard, :] = tile(gate[rows], k)
            low_half = down[2 * f * half : (2 * f + 1) * half]
            high_half = down[(2 * f + 1) * half : (2 * f + 2) * half]
            own_half = jnp.where(low, low_half, high_half)
            for k in range(pack.down_tiles):
                at = pack.down_at + k * pack.half_step
                out[f, at : at + half, :] = tile(own_half, k)
            for k in range(pack.out_tiles):
                at = pack.out_at + k * pack.shard_step
                other = k + pack.out_tiles
                high = tile(outward[rows], other) if other < pack.down_tiles else blank
                out[f, at : at + shard, :] = jnp.where(low, tile(outward[rows], k), high)
            if pack.used < pack.rows:
                out[f, pack.used :, :] = jnp.zeros((pack.rows - pack.used, LANES), BF)


def mlp_grads(pack, parts, idx, hid, e, mn, gm, gt, attn, mix, mg, after=()):
    rows, depth = e.shape
    ff = gm.shape[1]
    return call(
        functools.partial(mlp_grads_kernel, pack),
        (shape((parts, pack.rows, LANES), BF), shape((parts, pack.rows, LANES), BF)),
        [IN_SMEM] + [IN_VMEM] * 8,
        [],
        (idx, hid, e, mn, gm, gt, attn, mix, mg),
        2 * rows * depth * (3 * ff + depth),
        after,
        limit=40,
    )


def halves(idx, zero, one, got):
    first = idx[0] == 0
    keep = jnp.where(first, zero[...], one[...])
    other = got[...]
    return jnp.where(first, keep, other), jnp.where(first, other, keep)


def gain_of(last_tile, shard):
    return last_tile.astype(F32).T[LANES - HD : LANES - HD + 1, :shard]


def unpack_mlp_kernel(pack, idx, zero, one, got, gate_out, up_out, down_out, o_out, gain_out):
    shard, half = pack.shard, pack.half
    both = halves(idx, zero, one, got)
    for value, out in zip(both, (gate_out, up_out)):
        for k in range(pack.gate_tiles):
            at = k * pack.shard_step
            out[:, k * LANES : (k + 1) * LANES] = value[at : at + shard].astype(F32)
    depth = down_out.shape[0]
    downs = []
    for side, value in enumerate(both):
        tiles = []
        for k in range(pack.down_tiles):
            at = pack.down_at + k * pack.half_step
            tiles.append(value[at : at + half])
        downs.append(jnp.concatenate(tiles, axis=1).astype(F32))
    down_out[...] = jnp.concatenate(downs, axis=0).T[:depth]
    tiles = []
    for k in range(pack.down_tiles):
        at = pack.out_at + (k % pack.out_tiles) * pack.shard_step
        tiles.append(both[k // pack.out_tiles][at : at + shard])
    o_out[...] = jnp.concatenate(tiles, axis=1)[:, :depth].astype(F32)
    at = pack.out_at + (pack.down_tiles - 1 - pack.out_tiles) * pack.shard_step
    gain_out[...] = gain_of(both[1][at : at + pack.shard_step], shard)


def unpack_mlp(pack, idx, zero, one, got, ff, depth):
    return call(
        functools.partial(unpack_mlp_kernel, pack),
        (
            shape((pack.shard, ff), F32),
            shape((pack.shard, ff), F32),
            shape((depth, 2 * pack.half), F32),
            shape((pack.shard, depth), F32),
            shape((1, pack.shard), F32),
        ),
        [IN_SMEM] + [IN_VMEM] * 3,
        [],
        (idx, zero, one, got),
        1000,
        limit=24,
    )


def unpack_entry_kernel(pack, idx, zero, one, got, q_out, k_out, v_out, gain_out):
    shard = pack.shard
    tiles = []
    both = halves(idx, zero, one, got)
    for value in both:
        for k in range(pack.entry_tiles):
            at = k * pack.shard_step
            tiles.append(value[at : at + shard])
    full = jnp.concatenate(tiles, axis=1).astype(F32)
    qw, kw = HQ * HD, HK * HD
    q_out[...] = full[:, :qw]
    k_out[...] = full[:, qw : qw + kw]
    v_out[...] = full[:, qw + kw : qw + 2 * kw]
    at = (pack.entry_tiles - 1) * pack.shard_step
    gain_out[...] = gain_of(both[1][at : at + pack.shard_step], shard)


def unpack_entry(pack, idx, zero, one, got):
    qw, kw = HQ * HD, HK * HD
    return call(
        functools.partial(unpack_entry_kernel, pack),
        (
            shape((pack.shard, qw), F32),
            shape((pack.shard, kw), F32),
            shape((pack.shard, kw), F32),
            shape((1, pack.shard), F32),
        ),
        [IN_SMEM] + [IN_VMEM] * 3,
        [],
        (idx, zero, one, got),
        1000,
        limit=24,
    )


def attend_back_kernel(blocks, idx, q, ag, lse, *refs):
    kv = [r[...] for r in refs[:blocks]]
    dq_out, own_out = refs[blocks : blocks + 2]
    far_out = refs[blocks + 2 :]
    rows = q.shape[0]
    reach = idx[1]
    causal = causal_mask(rows)
    queries = q[...]
    grads = ag[...]
    dq_parts = []
    dk_parts = []
    dv_parts = []
    for g in range(HK):
        keys = [head(b, g) for b in kv]
        all_keys = jnp.concatenate(keys, axis=0)
        values = jnp.concatenate([head(b, HK + g) for b in kv], axis=0)
        dk = None
        dv = None
        for i in range(GROUP):
            h = g * GROUP + i
            query = head(queries, h)
            grad = head(grads, h)
            s = jnp.concatenate(
                [score_block(k, query, d, reach, causal) for d, k in enumerate(keys)], axis=0
            )
            p = jnp.exp(s - lse[h : h + 1, :])
            dp = nt(values, grad)
            delta = jnp.sum(p * dp, axis=0, keepdims=True)
            ds = (p * (dp - delta)).astype(BF)
            dv_h = nn(p.astype(BF), grad)
            dk_h = nn(ds, query)
            dk = dk_h if dk is None else dk + dk_h
            dv = dv_h if dv is None else dv + dv_h
            dq_parts.append(tn(ds, all_keys) * HD ** (-0.5))
        dk_parts.append(dk)
        dv_parts.append(dv)
    dq_out[...] = jnp.concatenate(dq_parts, axis=1)
    joined = jnp.concatenate(dk_parts + dv_parts, axis=1)
    own_out[...] = joined[:rows]
    for d, out in enumerate(far_out):
        out[...] = joined[(d + 1) * rows : (d + 2) * rows].astype(BF)


def attend_back(idx, q, ag, lse, kv, after=()):
    rows = q.shape[0]
    outs = [shape((rows, HQ * HD), F32), shape((rows, 2 * HK * HD), F32)]
    outs += [shape((rows, 2 * HK * HD), BF) for _ in kv[1:]]
    return call(
        functools.partial(attend_back_kernel, len(kv)),
        outs,
        [IN_SMEM] + [IN_VMEM] * (3 + len(kv)),
        [],
        (idx, q, ag, lse) + tuple(kv),
        5 * 2 * rows * rows * len(kv) * HQ * HD * 4,
        after,
    )


def input_back_kernel(layer, pack, far, idx, x, normed, dq, own_kv, *refs):
    far_kv = refs[:far]
    rg, a_own, a_got, v_own, v_got, cos, sin, ig_out, m_out, t_out, a_w, v_w, sems = refs[far:]
    own = idx[0] == layer
    first = idx[0] == 0
    fetch(own, a_own, a_got, a_w, sems.at[0])
    fetch(own, v_own, v_got, v_w, sems.at[1])
    kv = own_kv[...]
    for r in far_kv:
        kv = kv + r[...].astype(F32)
    half = HK * HD
    qk = jnp.concatenate([dq[...], kv[:, :half]], axis=1)
    qk_in = rot_back(qk, cos[...], sin[...]).astype(BF)
    v_in = kv[:, half:].astype(BF)
    rows, depth = x.shape
    width = (HQ + HK) * HD
    padded = jnp.concatenate([jnp.zeros((rows, HQ * HD), BF), v_in], axis=1)
    arrive(a_own, a_w, sems.at[0])
    arrive(v_own, v_w, sems.at[1])
    ng = nt(qk_in, a_w[:, :width]) + nt(padded, v_w[:, :width])
    z = x[...].astype(F32)
    gain = gain_row(a_w[:, width:])
    inv = norm_scale(z)
    weighted = ng * gain
    part = inv * weighted - z * (inv * inv * inv) * jnp.mean(z * weighted, axis=-1, keepdims=True)
    ig_out[...] = (rg[...] + part).astype(BF)
    nv = normed[...]
    grads = jnp.concatenate(
        [
            tn(nv, qk_in).astype(BF),
            tn(nv, v_in).astype(BF),
            gain_tile(ng * z * inv)[:, :HD],
        ],
        axis=1,
    )
    shard = pack.shard
    for f in range(m_out.shape[0]):
        piece = grads[f * shard : (f + 1) * shard]
        for k in range(pack.entry_tiles):
            at = k * pack.shard_step
            low = tile(piece, k)
            high = tile(piece, k + pack.entry_tiles)
            m_out[f, at : at + shard, :] = jnp.where(first, low, high)
            t_out[f, at : at + shard, :] = jnp.where(first, high, low)


def input_back(layer, pack, parts, idx, x, normed, dq, own_kv, far_kv, rg, weights, cos, sin, after=()):
    rows, depth = x.shape
    a_own, a_got, v_own, v_got = weights
    args = (idx, x, normed, dq, own_kv) + tuple(far_kv)
    args += (rg, a_own, a_got, v_own, v_got, cos, sin)
    packed = (parts, pack.entry_rows, LANES)
    return call(
        functools.partial(input_back_kernel, layer, pack, len(far_kv)),
        (shape((rows, depth), BF), shape(packed, BF), shape(packed, BF)),
        [IN_SMEM] + [IN_VMEM] * (5 + len(far_kv)) + [ANYWHERE] * 4 + [IN_VMEM] * 2,
        [pltpu.VMEM(a_own.shape, BF), pltpu.VMEM(v_own.shape, BF), pltpu.SemaphoreType.DMA((2,))],
        args,
        2 * 2 * rows * depth * 1536,
        after,
    )


def crossed(value, axis, mask):
    count = lax.axis_size(axis)
    return lax.ppermute(value, axis, [(i, i ^ mask) for i in range(count)])


def shifted(value, distance):
    devices = range(lax.axis_size("ctx"))
    return lax.ppermute(value, "ctx", [(i, i + distance) for i in devices if i + distance in devices])


def other_core(value):
    return crossed(value, "section", 1)


def bits_of(count):
    return [b for b in range(count.bit_length() - 1)]


def held(value, *deps):
    return lax.optimization_barrier((value,) + deps)[0]


def gather_step(value, have, bit, wait):
    me = lax.axis_index("fsdp")
    got = crossed(value, "fsdp", 1 << bit)
    if wait:
        got = held(got, *wait)
    low = ((me >> bit) & 1) == 0
    place = sum(1 for b in have if b > bit)
    return jnp.stack([jnp.where(low, value, got), jnp.where(low, got, value)], axis=place)


def gather_some(values, orders, first, last, wait=()):
    for step in range(first, last):
        late = wait if step == last - 1 else ()
        values = [gather_step(v, o[:step], o[step], late) for v, o in zip(values, orders)]
    return values


def whole_rows(value):
    return value.reshape((value.size // value.shape[-1],) + value.shape[-1:])


def cut(value, left, bit):
    mine = (lax.axis_index("fsdp") >> bit) & 1
    place = sorted(left, reverse=True).index(bit)
    send = lax.dynamic_index_in_dim(value, 1 - mine, place, keepdims=False)
    keep = lax.dynamic_index_in_dim(value, mine, place, keepdims=False)
    return send, keep


def added(halves, bit, wait=()):
    send, keep = halves
    got = crossed(send, "fsdp", 1 << bit)
    if wait:
        got = held(got, *wait)
    return (keep.astype(F32) + got.astype(F32)).astype(BF)


def first_cut(value, order):
    count = lax.axis_size("fsdp")
    value = value.reshape((2,) * len(order) + (value.shape[0] // count,) + value.shape[1:])
    return cut(value, order, order[0])


def scatter_rest(value, order, wait=()):
    for step in range(1, len(order)):
        late = wait if step == len(order) - 1 else ()
        value = added(cut(value, order[step:], order[step]), order[step], late)
    return value


def sum_over_ctx(value):
    count = lax.axis_size("ctx")
    if count & (count - 1):
        return lax.psum(value, "ctx")
    for bit in bits_of(count):
        value = (value.astype(F32) + crossed(value, "ctx", 1 << bit).astype(F32)).astype(BF)
    return value


def ctx_cut(value):
    me = lax.axis_index("ctx") & 1
    size = value.shape[0] // 2
    send = lax.dynamic_slice_in_dim(value, (1 - me) * size, size, 0)
    keep = lax.dynamic_slice_in_dim(value, me * size, size, 0)
    return send, keep


def ctx_begin(halves, wait=()):
    send, keep = halves
    got = crossed(send, "ctx", 1)
    if wait:
        got = held(got, *wait)
    return (keep.astype(F32) + got.astype(F32)).astype(BF)


def ctx_middle(value, wait=()):
    for bit in bits_of(lax.axis_size("ctx"))[1:]:
        value = added_over_ctx(value, bit, wait)
    return value


def ctx_end(value, wait=()):
    low = (lax.axis_index("ctx") & 1) == 0
    got = crossed(value, "ctx", 1)
    if wait:
        got = held(got, *wait)
    return jnp.concatenate([jnp.where(low, value, got), jnp.where(low, got, value)], axis=0)


def added_over_ctx(value, bit, wait):
    got = crossed(value, "ctx", 1 << bit)
    if wait:
        got = held(got, *wait)
    return (value.astype(F32) + got.astype(F32)).astype(BF)


def body(
    inputs,
    positions,
    out_grad,
    attn_gain,
    query_proj,
    key_proj,
    value_proj,
    out_proj,
    mlp_gain,
    gate_proj,
    up_proj,
    down_proj,
):
    core = lax.axis_index("section")
    first = core == 0
    ctx = lax.axis_index("ctx")
    ctx_count = lax.axis_size("ctx")
    fsdp_count = lax.axis_size("fsdp")
    micro, seqs, block, depth = inputs.shape
    shard = query_proj.shape[1]
    rows = seqs * block
    idx = jnp.stack([core, ctx]).astype(jnp.int32)
    up_order = bits_of(fsdp_count)
    down_order = up_order[::-1]

    def pick(a, b):
        return jnp.where(first, a, b)

    def tile_of(gain):
        return jnp.broadcast_to(gain[0][:, None], (shard, LANES))

    a_piece = jnp.concatenate([query_proj[0], key_proj[0], tile_of(attn_gain)], axis=1)
    v_piece = jnp.concatenate([out_proj[0], value_proj[0], tile_of(mlp_gain)], axis=1)
    steps = len(up_order)
    a_own, v_own = gather_some([a_piece, v_piece], [up_order, down_order], 0, steps)
    a_own = whole_rows(a_own)
    v_own = whole_rows(v_own)
    a_got = other_core(a_own)
    v_got = other_core(v_own)
    attn_w = (a_own, a_got, v_own, v_got)

    half = down_proj.shape[1] // 2
    g_keep = pick(gate_proj[0], up_proj[0])
    g_got = other_core(pick(up_proj[0], gate_proj[0]))
    wide_down = jnp.pad(down_proj[0], ((0, 0), (0, -depth % LANES)))
    d_keep = pick(wide_down[:half], wide_down[half:])
    d_got = other_core(pick(wide_down[half:], wide_down[:half]))
    def feed_forward_pieces(layer):
        g_piece = pick(g_keep, g_got) if layer == 0 else pick(g_got, g_keep)
        d_piece = pick(d_keep, d_got) if layer == 0 else pick(d_got, d_keep)
        return [g_piece, d_piece]

    parts_of_down = fsdp_count if half % 16 == 0 else 0

    def down_halves(mine, theirs):
        if parts_of_down:
            return (mine, theirs)
        mine, theirs = [v.reshape(fsdp_count, half, -1) for v in (mine, theirs)]
        full = jnp.stack([pick(mine, theirs), pick(theirs, mine)], axis=1)
        full = whole_rows(full)
        return (full, full)

    places = lax.dynamic_index_in_dim(positions, core, 0, keepdims=False).reshape(rows)
    frequency = rope_base ** (-(jnp.arange(HD // 2, dtype=F32) * 2.0 / HD))
    angles = places.astype(F32)[:, None] * frequency
    cos = jnp.concatenate([jnp.cos(angles)] * 4, axis=-1)
    sin = jnp.concatenate([jnp.sin(angles)] * 4, axis=-1)

    x = lax.dynamic_index_in_dim(inputs, core, 0, keepdims=False).reshape(rows, depth)
    saved = []
    ff_w = [None, None]
    for layer in range(2):
        normed, q, kv_own = attn_in(layer, idx, x, attn_w, cos, sin)
        kv = [kv_own] + [shifted(kv_own, d) for d in range(1, ctx_count)]
        orders = [up_order, down_order] if layer == 0 else [down_order, up_order]
        if layer == 0:
            parts = lax.optimization_barrier(tuple(feed_forward_pieces(0)) + (a_own, v_own))[:2]
        parts = gather_some(parts, orders, 0, 1, (normed,))
        if layer == 1:
            parts = lax.optimization_barrier(tuple(parts) + (normed,))[:2]
        g_all, d_all = gather_some(parts, orders, 1, steps)
        attn, lse = attend(idx, q, kv)
        g_all, d_all, attn = lax.optimization_barrier((whole_rows(g_all), whole_rows(d_all), attn))
        ff_w[layer] = (g_all, other_core(g_all)) + down_halves(d_all, other_core(d_all))
        if layer == 0:
            parts = lax.optimization_barrier(tuple(feed_forward_pieces(1)) + (g_all, d_all))[:2]
        y, resid, mn, gate, up, hid = mlp(layer, parts_of_down, idx, x, attn, attn_w, *ff_w[layer])
        saved.append((x, normed, q, kv, attn, lse, resid, mn, gate, up, hid))
        x = y
    outs = [saved[1][0], x]

    pack = Packing(shard, half, gate_proj.shape[2], depth)

    def joined(mine, theirs, wait=()):
        got = other_core(theirs)
        if wait:
            got = held(got, *wait)
        return (mine.astype(F32) + got.astype(F32)).astype(BF)

    e = lax.dynamic_index_in_dim(out_grad, core, 0, keepdims=False).reshape(rows, depth)
    entry = [None, None]
    def feed_forward_back(layer, e, after, between):
        x, normed, q, kv, attn, lse, resid, mn, gate, up, hid = saved[layer]
        gm, gt, rg, mix, ag, mg = mlp_back(
            layer, parts_of_down, idx, e, resid, gate, up, *ff_w[layer], attn_w, after
        )
        done = tuple(between(ag)) if between else ()
        mine, theirs = mlp_grads(pack, fsdp_count, idx, hid, e, mn, gm, gt, attn, mix, mg, done)
        return rg, ag, mine, theirs

    def attention_back(layer, ag, after):
        x, normed, q, kv, attn, lse, resid, mn, gate, up, hid = saved[layer]
        back = attend_back(idx, q, ag, lse, kv, after)
        far_kv = [shifted(part, -(d + 1)) for d, part in enumerate(back[2:])]
        return back[0], back[1], far_kv

    def entry_back(layer, dq, own_kv, far_kv, rg, after):
        x, normed = saved[layer][:2]
        e, mine, theirs = input_back(
            layer, pack, fsdp_count, idx, x, normed, dq, own_kv, far_kv, rg, attn_w, cos, sin, after
        )
        entry[layer] = e
        return e, mine, theirs

    orders = (up_order, down_order)

    def start(value, at):
        return [first_cut(value[:, :at], up_order), first_cut(value[:, at:], down_order)]

    def sends(cuts):
        return tuple(c[0] for c in cuts)

    def first_sums(cuts, wait):
        return [added(c, o[0], wait) for c, o in zip(cuts, orders)]

    def last_sums(values, wait):
        values = [scatter_rest(v, o, wait) for v, o in zip(values, orders)]
        return jnp.concatenate(values, axis=1)[0]

    def next_cuts(values):
        return [cut(v, o[1:], o[1]) for v, o in zip(values, orders)] if steps > 1 else [values]

    middle = pack.down_at
    entry_middle = pack.entry_rows // 2
    rg, ag, mine, theirs = feed_forward_back(1, e, (), None)
    dq, own_kv, far_kv = attention_back(1, ag, (mine,))
    m1 = start(joined(mine, theirs, (dq,)), middle)
    e, a_mine, a_theirs = entry_back(1, dq, own_kv, far_kv, rg, sends(m1))
    m1 = first_sums(m1, (e,))

    def between(ag):
        m1_cut.extend(ctx_cut(last_sums(m1, (ag,))))
        return m1_cut[:1]

    m1_cut = []
    rg, ag, mine, theirs = feed_forward_back(0, e, tuple(m1), between)
    m0 = start(joined(mine, theirs), middle)
    m1 = ctx_begin(m1_cut, (m0[0][0],))
    dq, own_kv, far_kv = attention_back(0, ag, sends(m0) + (m1,))
    a1 = start(joined(a_mine, a_theirs, (dq,)), entry_middle)
    m0 = first_sums(m0, (dq,))
    m1 = ctx_middle(m1, (far_kv[-1],))
    e, a_mine, a_theirs = entry_back(
        0, dq, own_kv, far_kv, rg, sends(next_cuts(m0)) + sends(a1) + (m1,)
    )
    a0 = start(joined(a_mine, a_theirs), entry_middle)
    late = sends(a0)[0]
    m1 = held(m1, late)
    m0 = ctx_cut(last_sums(m0, (late,)))
    a1 = first_sums(a1, (m0[0],))
    a0 = first_sums(a0, (m0[0],))
    m0 = ctx_begin(m0, tuple(a0))
    a1 = last_sums(a1, (m0,))
    a0 = last_sums(a0, (m0,))
    m1 = ctx_end(m1, (a0,))
    a0 = ctx_begin(ctx_cut(jnp.concatenate([a0, a1], axis=0)), ())
    m0 = ctx_middle(m0, (a0,))
    a0 = ctx_middle(a0, (m0,))
    a0 = ctx_end(a0)
    a0, a1 = a0[: pack.entry_rows], a0[pack.entry_rows :]

    def own_layer(zero, one):
        keep = pick(zero, one)
        got = other_core(pick(one, zero))
        return (pick(keep, got), pick(got, keep))

    outs[0], outs[1], entry[0], entry[1], _ = lax.optimization_barrier(
        (outs[0], outs[1], entry[0], entry[1], late)
    )
    section_out = jnp.stack(own_layer(outs[0], outs[1])).reshape(1, micro, seqs, block, depth)
    input_grad = jnp.stack(own_layer(entry[0], entry[1])).reshape(1, micro, seqs, block, depth)
    ff = gate_proj.shape[2]
    a_got = other_core(pick(a1, a0))
    query_g, key_g, value_g, attn_gain_g = unpack_entry(pack, idx, a0, a1, a_got)
    m0 = ctx_end(m0, (query_g, section_out, input_grad))
    m_got = other_core(pick(m1, m0))
    gate_g, up_g, down_g, out_g, mlp_gain_g = unpack_mlp(pack, idx, m0, m1, m_got, ff, depth)

    return (
        section_out,
        input_grad,
        attn_gain_g,
        query_g[None],
        key_g[None],
        value_g[None],
        out_g[None],
        mlp_gain_g,
        gate_g[None],
        up_g[None],
        down_g.T[None],
    )


def solution(mesh):
    rows = P(None, "fsdp", "ctx", None)
    both = P("section", None, "fsdp", "ctx", None)
    vec = P("section", "fsdp")
    mat = P("section", "fsdp", None)
    return jax.shard_map(
        body,
        mesh=mesh,
        in_specs=(rows, P(None, "fsdp", "ctx"), rows, vec, mat, mat, mat, mat, vec, mat, mat, mat),
        out_specs=(both, both, vec, mat, mat, mat, mat, vec, mat, mat, mat),
        check_vma=False,
    )
```
